32 devices in a mesh: grp: 2 (over core), gx: 8 (over z, y), gy: 2 (over x).
Axes of the slice: x: 2, y: 2, z: 4, core: 2. Of those that a mesh axis runs over, the one named last changes fastest.
Arguments:
- source: bfloat16 [4, 64, 128, 256], P(None, None, ('grp', 'gx'), 'gy'), may hold values from -6 to 6
- speed: bfloat16 [64, 128, 256], P(('grp', 'gx'), None, 'gy'), may hold values from 1 to 2.5
- impedance: bfloat16 [64, 128, 256], P(('grp', 'gx'), None, 'gy'), may hold values from 0.5 to 2
Outputs:
- pressure: float32 [64, 128, 256], P(('grp', 'gx'), None, 'gy')
- velocity: float32 [3, 64, 128, 256], P(None, ('grp', 'gx'), None, 'gy')
The draws below stay inside these ranges and needn't reach their ends.
All inputs are finite; a program needn't handle non-finite values.
Results may differ from the reference program's by a relative error of at most 0.0017.
Values may be sent and summed in bfloat16 or wider, within the bound.
No kernel may reach another device: no remote copies, remote signals or barrier semaphores. Data moves between devices by JAX's collectives and lax.ppermute only.
A program may use at most 128 MiB of HBM per device.

```python
import math
import jax
import jax.numpy as jnp
from jax import lax

STEPS = 4
NX = 64
NY = 128
NZ = 256


def steps_of(key, shape, shards, smallest, high):
    loudness = 1.0
    for position, shards_of in shards:
        steps = jax.random.uniform(jax.random.fold_in(jax.random.fold_in(key, 6), position), (shards_of,), jnp.float32, smallest / len(shards), high / len(shards))
        loudness = loudness * jnp.repeat(jnp.exp(steps), shape[position] // shards_of).reshape((-1,) + (1,) * (len(shape) - 1 - position))
    return loudness


def normal_values(stream_key, extent, scale, limit, pieces=(), held_as=jnp.bfloat16):
    loudness = steps_of(stream_key, extent, pieces, -0.22, 0.18) if pieces else 1.0
    drawn = jax.random.normal(stream_key, extent, jnp.float32) * scale * loudness
    return jnp.minimum(jnp.maximum(drawn, -limit), limit).astype(held_as)


def setup_inputs(seed: int = 0) -> dict:
    key_list = jax.random.split(jax.random.key(seed), 4)
    source = normal_values(key_list[0], (STEPS, NX, NY, NZ), 1.0, 6.0, ((2, 16), (3, 2)))
    speed = jnp.clip(jnp.exp(math.log(2.5) - 0.916290732 * jax.random.uniform(key_list[1], (NX, NY, NZ), jnp.float32) ** steps_of(key_list[1], (NX, NY, NZ), ((0, 16), (2, 2)), -0.2, 0.2)), 1.0, 2.5).astype(jnp.bfloat16)
    impedance = jnp.clip(jnp.exp(math.log(2.0) - 1.3862944 * jax.random.uniform(key_list[2], (NX, NY, NZ), jnp.float32) ** steps_of(key_list[2], (NX, NY, NZ), ((0, 16), (2, 2)), -0.2, 0.2)), 0.5, 2.0).astype(jnp.bfloat16)
    return dict(source=source, speed=speed, impedance=impedance)


courant = 0.15


def forward_diff(field, dim):
    widths = [(0, 0)] * field.ndim
    widths[dim] = (0, 1)
    padded = jnp.pad(field, widths)
    return lax.slice_in_dim(padded, 1, field.shape[dim] + 1, axis=dim) - field


def backward_diff(field, dim):
    widths = [(0, 0)] * field.ndim
    widths[dim] = (1, 0)
    padded = jnp.pad(field, widths)
    return field - lax.slice_in_dim(padded, 0, field.shape[dim], axis=dim)


def reference(source, speed, impedance):
    sound = speed.astype(jnp.float32)
    imped = impedance.astype(jnp.float32)
    stiff = sound * imped
    buoy = sound / imped
    pressure = jnp.zeros(speed.shape, jnp.float32)
    velocity = [jnp.zeros(speed.shape, jnp.float32) for _ in range(3)]
    for step in range(STEPS):
        pressure = pressure + source[STEPS - 1 - step].astype(jnp.float32)
        loaded = stiff * pressure
        velocity = [velocity[d] + courant * forward_diff(loaded, d) for d in range(3)]
        spread = backward_diff(buoy * velocity[0], 0) + backward_diff(buoy * velocity[1], 1)
        spread = spread + backward_diff(buoy * velocity[2], 2)
        pressure = pressure + courant * spread
    return pressure, jnp.stack(velocity)
```

```python
import functools

import jax
import jax.numpy as jnp
from jax import lax
from jax.experimental import pallas as pl
from jax.experimental.pallas import tpu as pltpu
from jax.sharding import PartitionSpec as P

courant = 0.15
EDGE = 4
STRIP = 4 * EDGE
LOW, HIGH = EDGE - 1, 3 * EDGE


def f32(x):
    return x.astype(jnp.float32)


def iota(shape, dim):
    return lax.broadcasted_iota(jnp.int32, shape, dim)


def brick_block(src, step, layer):
    bricks = f32(src[:, layer, step])
    return bricks.reshape(bricks.shape[0] * bricks.shape[1], bricks.shape[2])


def coefficients(speed, imped):
    held = imped > 0.0
    stiff = courant * (speed * imped)
    buoy = jnp.where(held, courant * (speed / jnp.where(held, imped, 1.0)), 0.0)
    return stiff, buoy


class Block:
    def __init__(self, shape, series):
        self.row, self.lane = iota(shape, 0), iota(shape, 1)
        self.rows, self.lanes = shape
        self.series = series

    def fwd_y(self, a):
        return jnp.where(self.row == self.rows - 1, 0.0, pltpu.roll(a, self.rows - 1, 0)) - a

    def bwd_y(self, g):
        return g - jnp.where(self.row == 0, 0.0, pltpu.roll(g, 1, 0))

    def column(self, key):
        j = key
        return self.series[:, j : j + 1]

    def fwd_z(self, a, key):
        col = self.column(key)
        return jnp.where(self.lane == self.lanes - 1, col, pltpu.roll(a, self.lanes - 1, 1)) - a

    def bwd_z(self, g, key):
        col = self.column(key)
        return g - jnp.where(self.lane == 0, col, pltpu.roll(g, 1, 1))


class Strip:
    def __init__(self, shape, series):
        self.lane = iota(shape, 1)
        self.rows, self.lanes = shape
        self.series = series

    def fwd_y(self, a):
        return jnp.where(self.lane == self.lanes - 1, 0.0, pltpu.roll(a, self.lanes - 1, 1)) - a

    def bwd_y(self, g):
        return g - jnp.where(self.lane == 0, 0.0, pltpu.roll(g, 1, 1))

    def fwd_z(self, a, key):
        self.series[key : key + 1, :] = a[HIGH : HIGH + 1, :]
        return pltpu.roll(a, self.rows - 1, 0) - a

    def bwd_z(self, g, key):
        self.series[key : key + 1, :] = g[LOW : LOW + 1, :]
        return g - pltpu.roll(g, 1, 0)


def load_key(step, layer):
    return step * 16 + layer


def flux_key(step, layer):
    return step * 16 + 8 + layer


def run_cut(space, steps, layers, src, stiff, buoy, pressure, velocity, put_load, put_flux):
    ends = (0, layers - 1)
    everywhere = tuple(range(layers))
    for k in range(steps):
        load = []
        for i in everywhere if k < steps - 1 else ends:
            p = src(k, i) if k == 0 else pressure[i] + src(k, i)
            pressure[i] = p
            load.append(stiff(i) * p)
        put_load(k, load[0])
        if k == steps - 1:
            put_flux(k, buoy(layers - 1) * (velocity[0, layers - 1] - load[-1]))
            return
        wanted = everywhere if k < steps - 2 else ends
        below = None
        for i in everywhere:
            x = (load[i + 1] - load[i]) if i + 1 < layers else -load[i]
            if k > 0:
                x = velocity[0, i] + x
            velocity[0, i] = x
            fx = buoy(i) * x
            if i == layers - 1:
                put_flux(k, fx)
            if i in wanted:
                y = space.fwd_y(load[i])
                z = space.fwd_z(load[i], load_key(k, i))
                if k > 0:
                    y, z = velocity[1, i] + y, velocity[2, i] + z
                velocity[1, i], velocity[2, i] = y, z
                spread = fx if i == 0 else fx - below
                spread = spread + space.bwd_y(buoy(i) * y)
                spread = spread + space.bwd_z(buoy(i) * z, flux_key(k, i))
                pressure[i] = pressure[i] + spread
            below = fx


def run_joined(space, steps, layers, src, stiff, buoy, pressure, velocity, load_in, flux_in, up, down):
    everywhere = tuple(range(layers))
    above, under = layers, layers + 1
    pa = xa = ya = za = pa2 = None
    pb = xb = yb = zb = pb2 = xb2 = None
    for k in range(steps):
        inner = 0 < k < steps - 1
        load = []
        for i in everywhere:
            p = src(k, i) if k == 0 else pressure[i] + src(k, i)
            pressure[i] = p
            load.append(stiff(i) * p)
        beyond = load_in(k)
        if k > 0:
            la = up[0] * pa
            beyond = beyond + la
            lb = down[0] * pb
        if inner:
            xa = -la if xa is None else xa - la
            if pa2 is not None:
                xa = xa + up[1] * pa2
            y, z = space.fwd_y(la), space.fwd_z(la, load_key(k, above))
            ya, za = (y, z) if ya is None else (ya + y, za + z)
            y, z = space.fwd_y(lb), space.fwd_z(lb, load_key(k, under))
            yb, zb = (y, z) if yb is None else (yb + y, zb + z)
            xb2 = lb if xb2 is None else xb2 + lb
            if pb2 is not None:
                xb2 = xb2 - down[1] * pb2
        xb = load[0] if k == 0 else xb + load[0] - lb
        fb = down[2] * xb
        below = flux_in(k) + fb
        for i in everywhere:
            x = (load[i + 1] if i + 1 < layers else beyond) - load[i]
            y = space.fwd_y(load[i])
            z = space.fwd_z(load[i], load_key(k, i))
            if k > 0:
                x, y, z = velocity[0, i] + x, velocity[1, i] + y, velocity[2, i] + z
            velocity[0, i], velocity[1, i], velocity[2, i] = x, y, z
            fx = buoy(i) * x
            spread = fx - below
            spread = spread + space.bwd_y(buoy(i) * y)
            spread = spread + space.bwd_z(buoy(i) * z, flux_key(k, i))
            pressure[i] = pressure[i] + spread
            below = fx
        if k == steps - 1:
            return
        if k == 0:
            pa, pb = -below, fb
            continue
        fa = up[2] * xa
        pa = pa + fa - below
        pa = pa + space.bwd_y(up[2] * ya) + space.bwd_z(up[2] * za, flux_key(k, above))
        fb2 = down[3] * xb2
        pb = pb + fb - fb2
        pb = pb + space.bwd_y(down[2] * yb) + space.bwd_z(down[2] * zb, flux_key(k, under))
        if k < steps - 2:
            pa2, pb2 = -fa, fb2


class Layers:
    def __init__(self, ref):
        self.ref = ref

    def __getitem__(self, i):
        return self.ref[i]

    def __setitem__(self, i, value):
        self.ref[i] = value


def pack_kernel(steps, layers, src, speed, imped, low, high):
    lanes = src.shape[-1]
    shape = (layers * EDGE, lanes)
    row, lane = iota(shape, 0), iota(shape, 1)
    for f in range(steps + 2):
        total = None
        for i in range(layers):
            mine = (row >> 2) == i
            picks = [mine & (lane == base + (row & 3)) for base in (0, lanes - EDGE)]
            pick = jnp.concatenate([jnp.where(p, 1.0, 0.0) for p in picks], 0).astype(jnp.bfloat16)
            if f < steps:
                block = brick_block(src, f, i).astype(jnp.bfloat16)
            else:
                block = (speed, imped)[f - steps][i]
            part = lax.dot_general(pick, block, (((1,), (1,)), ((), ())), preferred_element_type=jnp.float32)
            total = part if total is None else total + part
        rows = layers * EDGE
        low[f * rows : (f + 1) * rows, :] = total[:rows].astype(jnp.bfloat16)
        high[f * rows : (f + 1) * rows, :] = total[rows:].astype(jnp.bfloat16)


def strip_rows(message, at, lanes):
    parts = [f32(message[at + j * STRIP : at + (j + 1) * STRIP, :]) for j in range(lanes // 128)]
    return parts[0] if len(parts) == 1 else jnp.concatenate(parts, 1)


def put_strip(message, at, strip):
    for j in range(strip.shape[1] // 128):
        message[at + j * STRIP : at + (j + 1) * STRIP, :] = strip[:, j * 128 : (j + 1) * 128].astype(jnp.bfloat16)


def is_even():
    return lax.axis_index("gx") % 2 == 0


class Faces:
    def __init__(self, far, near):
        self.far, self.near = far, near
        self.even = is_even()

    def put(self, write, below, above):
        write(self.far, jnp.where(self.even, below, above))
        write(self.near, jnp.where(self.even, above, below))

    def above(self, read):
        return jnp.where(self.even, read(self.near), read(self.far))

    def below(self, read):
        return jnp.where(self.even, read(self.far), read(self.near))


class Series:
    def __init__(self, faces, write):
        self.faces, self.write, self.loads = faces, write, {}

    def put_load(self, k, a):
        self.loads[k] = a

    def put_flux(self, k, a):
        self.faces.put(lambda ref, value: self.write(ref, k, value), self.loads[k], a)


def rows_writer(rows):
    def write(ref, k, a):
        ref[k * rows : (k + 1) * rows, :] = a.astype(jnp.bfloat16)
    return write


def rows_reader(rows):
    return lambda k: lambda ref: f32(ref[k * rows : (k + 1) * rows, :])


def strip_layout(steps, y):
    step = STRIP * (y // 128)
    return step, steps * y, steps * y + steps * step


def prepare_kernel(steps, source, speed, imped, bricks, far, near, sems):
    copies = [pltpu.make_async_copy(source.at[k], bricks.at[:, k], sems.at[k]) for k in range(steps)]
    for copy in copies:
        copy.start()
    faces = Faces(far, near)
    last = speed.shape[0] - 1
    for j, ref in enumerate((speed, imped)):
        for depth in range(2):
            def write(out, value, at=2 * j + depth):
                out[at] = value.astype(jnp.bfloat16)
            faces.put(write, f32(ref[depth]), f32(ref[last - depth]))
    for copy in copies:
        copy.wait()


def cut_kernel(
    steps, layers, gy_size, src, speed, imped, low, high, left, right, far, near, strips,
    pressure, velocity, stiff_ref, buoy_ref, series, columns,
):
    y, lanes = speed.shape[1:]
    rows = layers * EDGE
    me = lax.axis_index("gy")
    square = (layers * STRIP, layers * STRIP)
    r, c = iota(square, 0), iota(square, 1)
    group = (r >> 2) & 3
    wanted = c == group * rows + (r >> 4) * EDGE + (r & 3)
    wanted = wanted & jnp.logical_not((group == 0) & (me == 0))
    wanted = wanted & jnp.logical_not((group == 3) & (me == gy_size - 1))
    order = jnp.where(wanted, 1.0, 0.0).astype(jnp.bfloat16)
    for f in range(steps + 2):
        parts = jnp.concatenate([a[f * rows : (f + 1) * rows, :] for a in (left, low, high, right)], 0)
        strips[f] = jnp.dot(order, parts, preferred_element_type=jnp.float32)

    def strip(f, i):
        return strips[f, i * STRIP : (i + 1) * STRIP, :]

    faces = Faces(far, near)
    step, base, extra = strip_layout(steps, y)
    last = layers - 1
    for j, (f, depth) in enumerate(((steps, 0), (steps, 1), (steps + 1, 0), (steps + 1, 1))):
        faces.put(
            lambda ref, value, at=extra + j * step: put_strip(ref, at, value), strip(f, depth), strip(f, last - depth)
        )

    coef = [coefficients(strip(steps, i), strip(steps + 1, i)) for i in range(layers)]
    series[...] = jnp.zeros(series.shape, jnp.float32)
    out = Series(faces, lambda ref, k, a: put_strip(ref, base + k * step, a))
    run_cut(
        Strip((STRIP, y), series), steps, layers, lambda k, i: strip(steps - 1 - k, i),
        lambda i: coef[i][0], lambda i: coef[i][1], {}, {}, out.put_load, out.put_flux,
    )
    columns[...] = series[...].T

    for i in range(layers):
        stiff_ref[i], buoy_ref[i] = coefficients(f32(speed[i]), f32(imped[i]))
    out = Series(faces, rows_writer(y))
    run_cut(
        Block((y, lanes), columns), steps, layers, lambda k, i: brick_block(src, steps - 1 - k, i),
        lambda i: stiff_ref[i], lambda i: buoy_ref[i], Layers(pressure), Layers(velocity), out.put_load, out.put_flux,
    )


def joined_kernel(
    steps, layers, src, speed, imped, strips, far, near, coef_far, coef_near,
    pressure, velocity, stiff_ref, buoy_ref, series, columns,
):
    y, lanes = speed.shape[1:]

    def strip(f, i):
        return strips[f, i * STRIP : (i + 1) * STRIP, :]

    faces = Faces(far, near)
    step, base, extra = strip_layout(steps, y)

    def strip_at(at):
        return lambda ref: strip_rows(ref, at, y)

    def beside(side, at):
        s = [side(at(j)) for j in range(4)]
        (stiff, buoy), (stiff2, buoy2) = coefficients(s[0], s[2]), coefficients(s[1], s[3])
        return stiff, stiff2, buoy, buoy2

    coef = [coefficients(strip(steps, i), strip(steps + 1, i)) for i in range(layers)]
    series[...] = jnp.zeros(series.shape, jnp.float32)
    run_joined(
        Strip((STRIP, y), series), steps, layers, lambda k, i: strip(steps - 1 - k, i),
        lambda i: coef[i][0], lambda i: coef[i][1], {}, {},
        lambda k: faces.above(strip_at(base + k * step)), lambda k: faces.below(strip_at(base + k * step)),
        beside(faces.above, lambda j: strip_at(extra + j * step)),
        beside(faces.below, lambda j: strip_at(extra + j * step)),
    )
    columns[...] = series[...].T

    for i in range(layers):
        stiff_ref[i], buoy_ref[i] = coefficients(f32(speed[i]), f32(imped[i]))
    held = Faces(coef_far, coef_near)
    read = rows_reader(y)
    run_joined(
        Block((y, lanes), columns), steps, layers, lambda k, i: brick_block(src, steps - 1 - k, i),
        lambda i: stiff_ref[i], lambda i: buoy_ref[i], Layers(pressure), Layers(velocity),
        lambda k: faces.above(read(k)), lambda k: faces.below(read(k)),
        beside(held.above, lambda j: lambda ref: f32(ref[j])),
        beside(held.below, lambda j: lambda ref: f32(ref[j])),
    )


def shifted(block, axis, distance):
    devices = range(lax.axis_size(axis))
    return lax.ppermute(block, axis, [(i, i + distance) for i in devices if i + distance in devices])


def swapped(block, axis, first):
    pairs = [(i, i + 1) for i in range(first, lax.axis_size(axis) - 1, 2)]
    return lax.ppermute(block, axis, pairs + [(j, i) for i, j in pairs])


def on_device(source, speed, impedance):
    steps, whole_x, brick_y, lanes = source.shape
    layers, y, _ = speed.shape
    assert layers == steps == EDGE and lanes == 128 and y % 128 == 0
    gy_size = lax.axis_size("gy")
    xs = ("grp", "gx")
    bf16 = jnp.bfloat16
    params = pltpu.CompilerParams(vmem_limit_bytes=32 * 1024 * 1024)
    sds = jax.ShapeDtypeStruct

    assert lax.axis_size("gx") % 2 == 0
    coef = sds((4, y, lanes), bf16)
    bricks, coef_far, coef_near = pl.pallas_call(
        functools.partial(prepare_kernel, steps),
        in_specs=[pl.BlockSpec(memory_space=pl.ANY)] + [pl.BlockSpec(memory_space=pltpu.VMEM)] * 2,
        out_shape=(sds((whole_x, steps, brick_y, lanes), bf16), coef, coef),
        scratch_shapes=[pltpu.SemaphoreType.DMA((steps,))],
        compiler_params=params,
        name="prepare",
    )(source, speed, impedance)
    coef_far, coef_near = swapped(coef_far, xs, 1), swapped(coef_near, xs, 0)
    relaid = lax.all_to_all(bricks, xs, split_axis=0, concat_axis=0, tiled=True)
    relaid = relaid.reshape(whole_x // layers, layers, steps, brick_y, lanes)
    relaid, coef_far, coef_near = lax.optimization_barrier((relaid, coef_far, coef_near))

    edge = sds(((steps + 2) * layers * EDGE, y), bf16)
    low, high = pl.pallas_call(
        functools.partial(pack_kernel, steps, layers), out_shape=(edge, edge), compiler_params=params, name="pack"
    )(relaid, speed, impedance)
    if gy_size == 2:
        left = right = lax.ppermute(jnp.where(lax.axis_index("gy") == 0, high, low), "gy", [(0, 1), (1, 0)])
    else:
        left, right = shifted(high, "gy", 1), shifted(low, "gy", -1)

    whole = pltpu.VMEM((layers, y, lanes), jnp.float32)
    series = [pltpu.VMEM((128, y), jnp.float32), pltpu.VMEM((y, 128), jnp.float32)]
    message = sds((steps * y + (steps + 4) * STRIP * (y // 128), 128), bf16)
    far, near, strips = pl.pallas_call(
        functools.partial(cut_kernel, steps, layers, gy_size),
        out_shape=(message, message, sds((steps + 2, layers * STRIP, y), jnp.float32)),
        scratch_shapes=[whole, pltpu.VMEM((3, layers, y, lanes), jnp.float32), whole, whole] + series,
        compiler_params=params,
        name="cut",
    )(relaid, speed, impedance, low, high, left, right)

    far, near = swapped(far, xs, 1), swapped(near, xs, 0)

    return pl.pallas_call(
        functools.partial(joined_kernel, steps, layers),
        out_shape=(sds((layers, y, lanes), jnp.float32), sds((3, layers, y, lanes), jnp.float32)),
        scratch_shapes=[whole, whole] + series,
        compiler_params=params,
        name="joined",
    )(relaid, speed, impedance, strips, far, near, coef_far, coef_near)


def solution(mesh):
    in_specs = (
        P(None, None, ("grp", "gx"), "gy"),
        P(("grp", "gx"), None, "gy"),
        P(("grp", "gx"), None, "gy"),
    )
    out_specs = (P(("grp", "gx"), None, "gy"), P(None, ("grp", "gx"), None, "gy"))
    return jax.shard_map(
        on_device, mesh=mesh, in_specs=in_specs, out_specs=out_specs, check_vma=False
    )
```

```python
import functools

import jax
import jax.numpy as jnp
from jax import lax
from jax.experimental import pallas as pl
from jax.experimental.pallas import tpu as pltpu
from jax.sharding import PartitionSpec as P

courant = 0.15
EDGE = 4
STRIP = 4 * EDGE
LOW, HIGH = EDGE - 1, 3 * EDGE


def f32(x):
    return x.astype(jnp.float32)


def iota(shape, dim):
    return lax.broadcasted_iota(jnp.int32, shape, dim)


def brick_block(src, step, layer):
    bricks = f32(src[:, layer, step])
    return bricks.reshape(bricks.shape[0] * bricks.shape[1], bricks.shape[2])


def coefficients(speed, imped):
    held = imped > 0.0
    stiff = courant * (speed * imped)
    buoy = jnp.where(held, courant * (speed / jnp.where(held, imped, 1.0)), 0.0)
    return stiff, buoy


class Block:
    def __init__(self, shape, series):
        self.row, self.lane = iota(shape, 0), iota(shape, 1)
        self.rows, self.lanes = shape
        self.series = series

    def fwd_y(self, a):
        return jnp.where(self.row == self.rows - 1, 0.0, pltpu.roll(a, self.rows - 1, 0)) - a

    def bwd_y(self, g):
        return g - jnp.where(self.row == 0, 0.0, pltpu.roll(g, 1, 0))

    def column(self, key):
        j = key
        return self.series[:, j : j + 1]

    def fwd_z(self, a, key):
        col = self.column(key)
        return jnp.where(self.lane == self.lanes - 1, col, pltpu.roll(a, self.lanes - 1, 1)) - a

    def bwd_z(self, g, key):
        col = self.column(key)
        return g - jnp.where(self.lane == 0, col, pltpu.roll(g, 1, 1))


class Strip:
    def __init__(self, shape, series):
        self.lane = iota(shape, 1)
        self.rows, self.lanes = shape
        self.series = series

    def fwd_y(self, a):
        return jnp.where(self.lane == self.lanes - 1, 0.0, pltpu.roll(a, self.lanes - 1, 1)) - a

    def bwd_y(self, g):
        return g - jnp.where(self.lane == 0, 0.0, pltpu.roll(g, 1, 1))

    def fwd_z(self, a, key):
        self.series[key : key + 1, :] = a[HIGH : HIGH + 1, :]
        return pltpu.roll(a, self.rows - 1, 0) - a

    def bwd_z(self, g, key):
        self.series[key : key + 1, :] = g[LOW : LOW + 1, :]
        return g - pltpu.roll(g, 1, 0)


def load_key(step, layer):
    return step * 16 + layer


def flux_key(step, layer):
    return step * 16 + 8 + layer


def run_cut(space, steps, layers, src, stiff, buoy, pressure, velocity, put_load, put_flux):
    ends = (0, layers - 1)
    everywhere = tuple(range(layers))
    for k in range(steps):
        load = []
        for i in everywhere if k < steps - 1 else ends:
            p = src(k, i) if k == 0 else pressure[i] + src(k, i)
            pressure[i] = p
            load.append(stiff(i) * p)
        put_load(k, load[0])
        if k == steps - 1:
            put_flux(k, buoy(layers - 1) * (velocity[0, layers - 1] - load[-1]))
            return
        wanted = everywhere if k < steps - 2 else ends
        below = None
        for i in everywhere:
            x = (load[i + 1] - load[i]) if i + 1 < layers else -load[i]
            if k > 0:
                x = velocity[0, i] + x
            velocity[0, i] = x
            fx = buoy(i) * x
            if i == layers - 1:
                put_flux(k, fx)
            if i in wanted:
                y = space.fwd_y(load[i])
                z = space.fwd_z(load[i], load_key(k, i))
                if k > 0:
                    y, z = velocity[1, i] + y, velocity[2, i] + z
                velocity[1, i], velocity[2, i] = y, z
                spread = fx if i == 0 else fx - below
                spread = spread + space.bwd_y(buoy(i) * y)
                spread = spread + space.bwd_z(buoy(i) * z, flux_key(k, i))
                pressure[i] = pressure[i] + spread
            below = fx


def run_joined(space, steps, layers, src, stiff, buoy, pressure, velocity, load_in, flux_in, up, down):
    everywhere = tuple(range(layers))
    above, under = layers, layers + 1
    pa = xa = ya = za = pa2 = None
    pb = xb = yb = zb = pb2 = xb2 = None
    for k in range(steps):
        inner = 0 < k < steps - 1
        load = []
        for i in everywhere:
            p = src(k, i) if k == 0 else pressure[i] + src(k, i)
            pressure[i] = p
            load.append(stiff(i) * p)
        beyond = load_in(k)
        if k > 0:
            la = up[0] * pa
            beyond = beyond + la
            lb = down[0] * pb
        if inner:
            xa = -la if xa is None else xa - la
            if pa2 is not None:
                xa = xa + up[1] * pa2
            y, z = space.fwd_y(la), space.fwd_z(la, load_key(k, above))
            ya, za = (y, z) if ya is None else (ya + y, za + z)
            y, z = space.fwd_y(lb), space.fwd_z(lb, load_key(k, under))
            yb, zb = (y, z) if yb is None else (yb + y, zb + z)
            xb2 = lb if xb2 is None else xb2 + lb
            if pb2 is not None:
                xb2 = xb2 - down[1] * pb2
        xb = load[0] if k == 0 else xb + load[0] - lb
        fb = down[2] * xb
        below = flux_in(k) + fb
        for i in everywhere:
            x = (load[i + 1] if i + 1 < layers else beyond) - load[i]
            y = space.fwd_y(load[i])
            z = space.fwd_z(load[i], load_key(k, i))
            if k > 0:
                x, y, z = velocity[0, i] + x, velocity[1, i] + y, velocity[2, i] + z
            velocity[0, i], velocity[1, i], velocity[2, i] = x, y, z
            fx = buoy(i) * x
            spread = fx - below
            spread = spread + space.bwd_y(buoy(i) * y)
            spread = spread + space.bwd_z(buoy(i) * z, flux_key(k, i))
            pressure[i] = pressure[i] + spread
            below = fx
        if k == steps - 1:
            return
        if k == 0:
            pa, pb = -below, fb
            continue
        fa = up[2] * xa
        pa = pa + fa - below
        pa = pa + space.bwd_y(up[2] * ya) + space.bwd_z(up[2] * za, flux_key(k, above))
        fb2 = down[3] * xb2
        pb = pb + fb - fb2
        pb = pb + space.bwd_y(down[2] * yb) + space.bwd_z(down[2] * zb, flux_key(k, under))
        if k < steps - 2:
            pa2, pb2 = -fa, fb2


class Layers:
    def __init__(self, ref):
        self.ref = ref

    def __getitem__(self, i):
        return self.ref[i]

    def __setitem__(self, i, value):
        self.ref[i] = value


def pack_kernel(steps, layers, src, speed, imped, low, high):
    lanes = src.shape[-1]
    shape = (layers * EDGE, lanes)
    row, lane = iota(shape, 0), iota(shape, 1)
    for f in range(steps + 2):
        total = None
        for i in range(layers):
            mine = (row >> 2) == i
            picks = [mine & (lane == base + (row & 3)) for base in (0, lanes - EDGE)]
            pick = jnp.concatenate([jnp.where(p, 1.0, 0.0) for p in picks], 0).astype(jnp.bfloat16)
            if f < steps:
                block = brick_block(src, f, i).astype(jnp.bfloat16)
            else:
                block = (speed, imped)[f - steps][i]
            part = lax.dot_general(pick, block, (((1,), (1,)), ((), ())), preferred_element_type=jnp.float32)
            total = part if total is None else total + part
        rows = layers * EDGE
        low[f * rows : (f + 1) * rows, :] = total[:rows].astype(jnp.bfloat16)
        high[f * rows : (f + 1) * rows, :] = total[rows:].astype(jnp.bfloat16)


def strip_rows(message, at, lanes):
    parts = [f32(message[at + j * STRIP : at + (j + 1) * STRIP, :]) for j in range(lanes // 128)]
    return parts[0] if len(parts) == 1 else jnp.concatenate(parts, 1)


def put_strip(message, at, strip):
    for j in range(strip.shape[1] // 128):
        message[at + j * STRIP : at + (j + 1) * STRIP, :] = strip[:, j * 128 : (j + 1) * 128].astype(jnp.bfloat16)


def is_even():
    return lax.axis_index("gx") % 2 == 0


class Faces:
    def __init__(self, far, near):
        self.far, self.near = far, near
        self.even = is_even()

    def put(self, write, below, above):
        write(self.far, jnp.where(self.even, below, above))
        write(self.near, jnp.where(self.even, above, below))

    def above(self, read):
        return jnp.where(self.even, read(self.near), read(self.far))

    def below(self, read):
        return jnp.where(self.even, read(self.far), read(self.near))


class Series:
    def __init__(self, faces, write):
        self.faces, self.write, self.loads = faces, write, {}

    def put_load(self, k, a):
        self.loads[k] = a

    def put_flux(self, k, a):
        self.faces.put(lambda ref, value: self.write(ref, k, value), self.loads[k], a)


def rows_writer(rows):
    def write(ref, k, a):
        ref[k * rows : (k + 1) * rows, :] = a.astype(jnp.bfloat16)
    return write


def rows_reader(rows):
    return lambda k: lambda ref: f32(ref[k * rows : (k + 1) * rows, :])


def strip_layout(steps, y):
    step = STRIP * (y // 128)
    return step, steps * y, steps * y + steps * step


def coefficients_kernel(speed, imped, stiff, buoy):
    for i in range(speed.shape[0]):
        stiff[i], buoy[i] = coefficients(f32(speed[i]), f32(imped[i]))


def cut_kernel(
    steps, layers, gy_size, src, stiff, buoy, low, high, left, right, far, near, strips,
    pressure, velocity, series, columns,
):
    y, lanes = stiff.shape[1:]
    rows = layers * EDGE
    me = lax.axis_index("gy")
    square = (layers * STRIP, layers * STRIP)
    r, c = iota(square, 0), iota(square, 1)
    group = (r >> 2) & 3
    wanted = c == group * rows + (r >> 4) * EDGE + (r & 3)
    wanted = wanted & jnp.logical_not((group == 0) & (me == 0))
    wanted = wanted & jnp.logical_not((group == 3) & (me == gy_size - 1))
    order = jnp.where(wanted, 1.0, 0.0).astype(jnp.bfloat16)
    for f in range(steps + 2):
        parts = jnp.concatenate([a[f * rows : (f + 1) * rows, :] for a in (left, low, high, right)], 0)
        strips[f] = jnp.dot(order, parts, preferred_element_type=jnp.float32)

    def strip(f, i):
        return strips[f, i * STRIP : (i + 1) * STRIP, :]

    faces = Faces(far, near)
    step, base, extra = strip_layout(steps, y)
    last = layers - 1
    for j, (f, depth) in enumerate(((steps, 0), (steps, 1), (steps + 1, 0), (steps + 1, 1))):
        faces.put(
            lambda ref, value, at=extra + j * step: put_strip(ref, at, value), strip(f, depth), strip(f, last - depth)
        )

    coef = [coefficients(strip(steps, i), strip(steps + 1, i)) for i in range(layers)]
    series[...] = jnp.zeros(series.shape, jnp.float32)
    out = Series(faces, lambda ref, k, a: put_strip(ref, base + k * step, a))
    run_cut(
        Strip((STRIP, y), series), steps, layers, lambda k, i: strip(steps - 1 - k, i),
        lambda i: coef[i][0], lambda i: coef[i][1], {}, {}, out.put_load, out.put_flux,
    )
    columns[...] = series[...].T

    out = Series(faces, rows_writer(y))
    run_cut(
        Block((y, lanes), columns), steps, layers, lambda k, i: brick_block(src, steps - 1 - k, i),
        lambda i: stiff[i], lambda i: buoy[i], Layers(pressure), Layers(velocity), out.put_load, out.put_flux,
    )


def joined_kernel(
    steps, layers, src, stiff, buoy, strips, far, near, coef_far, coef_near,
    pressure, velocity, series, columns,
):
    y, lanes = stiff.shape[1:]

    def strip(f, i):
        return strips[f, i * STRIP : (i + 1) * STRIP, :]

    faces = Faces(far, near)
    step, base, extra = strip_layout(steps, y)

    def strip_at(at):
        return lambda ref: strip_rows(ref, at, y)

    def beside(side, at):
        s = [side(at(j)) for j in range(4)]
        (stiff, buoy), (stiff2, buoy2) = coefficients(s[0], s[2]), coefficients(s[1], s[3])
        return stiff, stiff2, buoy, buoy2

    coef = [coefficients(strip(steps, i), strip(steps + 1, i)) for i in range(layers)]
    series[...] = jnp.zeros(series.shape, jnp.float32)
    run_joined(
        Strip((STRIP, y), series), steps, layers, lambda k, i: strip(steps - 1 - k, i),
        lambda i: coef[i][0], lambda i: coef[i][1], {}, {},
        lambda k: faces.above(strip_at(base + k * step)), lambda k: faces.below(strip_at(base + k * step)),
        beside(faces.above, lambda j: strip_at(extra + j * step)),
        beside(faces.below, lambda j: strip_at(extra + j * step)),
    )
    columns[...] = series[...].T

    held = Faces(coef_far, coef_near)
    read = rows_reader(y)
    run_joined(
        Block((y, lanes), columns), steps, layers, lambda k, i: brick_block(src, steps - 1 - k, i),
        lambda i: stiff[i], lambda i: buoy[i], Layers(pressure), Layers(velocity),
        lambda k: faces.above(read(k)), lambda k: faces.below(read(k)),
        beside(held.above, lambda j: lambda ref: f32(ref[j])),
        beside(held.below, lambda j: lambda ref: f32(ref[j])),
    )


def shifted(block, axis, distance):
    devices = range(lax.axis_size(axis))
    return lax.ppermute(block, axis, [(i, i + distance) for i in devices if i + distance in devices])


def swapped(block, axis, first):
    pairs = [(i, i + 1) for i in range(first, lax.axis_size(axis) - 1, 2)]
    return lax.ppermute(block, axis, pairs + [(j, i) for i, j in pairs])


def on_device(source, speed, impedance):
    steps, whole_x, brick_y, lanes = source.shape
    layers, y, _ = speed.shape
    assert layers == steps == EDGE and lanes == 128 and y % 128 == 0
    gy_size = lax.axis_size("gy")
    xs = ("grp", "gx")
    bf16 = jnp.bfloat16
    params = pltpu.CompilerParams(vmem_limit_bytes=32 * 1024 * 1024)
    sds = jax.ShapeDtypeStruct

    assert lax.axis_size("gx") % 2 == 0
    below = jnp.concatenate([speed[:2], impedance[:2]], 0)
    above = jnp.concatenate([speed[-1:], speed[-2:-1], impedance[-1:], impedance[-2:-1]], 0)
    even = is_even()
    coef_far, coef_near = jnp.where(even, below, above), jnp.where(even, above, below)
    coef_far, coef_near = swapped(coef_far, xs, 1), swapped(coef_near, xs, 0)
    relaid = lax.all_to_all(source.transpose(1, 0, 2, 3), xs, split_axis=0, concat_axis=0, tiled=True)
    relaid = relaid.reshape(whole_x // layers, layers, steps, brick_y, lanes)
    field = sds((layers, y, lanes), jnp.float32)
    stiff, buoy = pl.pallas_call(
        coefficients_kernel, out_shape=(field, field), compiler_params=params, name="coefficients"
    )(speed, impedance)
    relaid, coef_far, coef_near, stiff, buoy = lax.optimization_barrier((relaid, coef_far, coef_near, stiff, buoy))

    edge = sds(((steps + 2) * layers * EDGE, y), bf16)
    low, high = pl.pallas_call(
        functools.partial(pack_kernel, steps, layers), out_shape=(edge, edge), compiler_params=params, name="pack"
    )(relaid, speed, impedance)
    if gy_size == 2:
        left = right = lax.ppermute(jnp.where(lax.axis_index("gy") == 0, high, low), "gy", [(0, 1), (1, 0)])
    else:
        left, right = shifted(high, "gy", 1), shifted(low, "gy", -1)

    series = [pltpu.VMEM((128, y), jnp.float32), pltpu.VMEM((y, 128), jnp.float32)]
    message = sds((steps * y + (steps + 4) * STRIP * (y // 128), 128), bf16)
    far, near, strips = pl.pallas_call(
        functools.partial(cut_kernel, steps, layers, gy_size),
        out_shape=(message, message, sds((steps + 2, layers * STRIP, y), jnp.float32)),
        scratch_shapes=[pltpu.VMEM((layers, y, lanes), jnp.float32), pltpu.VMEM((3, layers, y, lanes), jnp.float32)] + series,
        compiler_params=params,
        name="cut",
    )(relaid, stiff, buoy, low, high, left, right)

    far, near = swapped(far, xs, 1), swapped(near, xs, 0)

    return pl.pallas_call(
        functools.partial(joined_kernel, steps, layers),
        out_shape=(field, sds((3, layers, y, lanes), jnp.float32)),
        scratch_shapes=series,
        compiler_params=params,
        name="joined",
    )(relaid, stiff, buoy, strips, far, near, coef_far, coef_near)


def solution(mesh):
    in_specs = (
        P(None, None, ("grp", "gx"), "gy"),
        P(("grp", "gx"), None, "gy"),
        P(("grp", "gx"), None, "gy"),
    )
    out_specs = (P(("grp", "gx"), None, "gy"), P(None, ("grp", "gx"), None, "gy"))
    return jax.shard_map(
        on_device, mesh=mesh, in_specs=in_specs, out_specs=out_specs, check_vma=False
    )
```

```python
import functools

import jax
import jax.numpy as jnp
from jax import lax
from jax.experimental import pallas as pl
from jax.experimental.pallas import tpu as pltpu
from jax.sharding import PartitionSpec as P

courant = 0.15
EDGE = 4
STRIP = 4 * EDGE
OWN = 3 * EDGE
WIDE = 2 * (OWN + EDGE)
LOW, HIGH = EDGE - 1, 3 * EDGE


def f32(x):
    return x.astype(jnp.float32)


def iota(shape, dim):
    return lax.broadcasted_iota(jnp.int32, shape, dim)


def brick_block(src, step, layer):
    bricks = f32(src[:, layer, step])
    return bricks.reshape(bricks.shape[0] * bricks.shape[1], bricks.shape[2])


def coefficients(speed, imped):
    held = imped > 0.0
    stiff = courant * (speed * imped)
    buoy = jnp.where(held, courant * (speed / jnp.where(held, imped, 1.0)), 0.0)
    return stiff, buoy


class Block:
    def __init__(self, shape, series):
        self.row, self.lane = iota(shape, 0), iota(shape, 1)
        self.rows, self.lanes = shape
        self.series = series

    def fwd_y(self, a):
        return jnp.where(self.row == self.rows - 1, 0.0, pltpu.roll(a, self.rows - 1, 0)) - a

    def bwd_y(self, g):
        return g - jnp.where(self.row == 0, 0.0, pltpu.roll(g, 1, 0))

    def column(self, key):
        return 0.0 if self.series is None else self.series[:, key : key + 1]

    def fwd_z(self, a, key):
        col = self.column(key)
        return jnp.where(self.lane == self.lanes - 1, col, pltpu.roll(a, self.lanes - 1, 1)) - a

    def bwd_z(self, g, key):
        col = self.column(key)
        return g - jnp.where(self.lane == 0, col, pltpu.roll(g, 1, 1))


class Strip:
    def __init__(self, shape, series):
        self.lane = iota(shape, 1)
        self.rows, self.lanes = shape
        self.series = series

    def fwd_y(self, a):
        return jnp.where(self.lane == self.lanes - 1, 0.0, pltpu.roll(a, self.lanes - 1, 1)) - a

    def bwd_y(self, g):
        return g - jnp.where(self.lane == 0, 0.0, pltpu.roll(g, 1, 1))

    def fwd_z(self, a, key):
        if self.series is not None:
            self.series[key : key + 1, :] = a[HIGH : HIGH + 1, :]
        return pltpu.roll(a, self.rows - 1, 0) - a

    def bwd_z(self, g, key):
        if self.series is not None:
            self.series[key : key + 1, :] = g[LOW : LOW + 1, :]
        return g - pltpu.roll(g, 1, 0)


def load_key(step, layer):
    return step * 16 + layer


def flux_key(step, layer):
    return step * 16 + 8 + layer


def run_cut(space, steps, layers, src, stiff, buoy, pressure, velocity, put_load, put_flux):
    ends = (0, layers - 1)
    everywhere = tuple(range(layers))
    for k in range(steps):
        load = []
        for i in everywhere if k < steps - 1 else ends:
            p = src(k, i) if k == 0 else pressure[i] + src(k, i)
            pressure[i] = p
            load.append(stiff(i) * p)
        put_load(k, load[0])
        if k == steps - 1:
            put_flux(k, buoy(layers - 1) * (velocity[0, layers - 1] - load[-1]))
            return
        wanted = everywhere if k < steps - 2 else ends
        below = None
        for i in everywhere:
            x = (load[i + 1] - load[i]) if i + 1 < layers else -load[i]
            if k > 0:
                x = velocity[0, i] + x
            velocity[0, i] = x
            fx = buoy(i) * x
            if i == layers - 1:
                put_flux(k, fx)
            if i in wanted:
                y = space.fwd_y(load[i])
                z = space.fwd_z(load[i], load_key(k, i))
                if k > 0:
                    y, z = velocity[1, i] + y, velocity[2, i] + z
                velocity[1, i], velocity[2, i] = y, z
                spread = fx if i == 0 else fx - below
                spread = spread + space.bwd_y(buoy(i) * y)
                spread = spread + space.bwd_z(buoy(i) * z, flux_key(k, i))
                pressure[i] = pressure[i] + spread
            below = fx


def run_joined(space, steps, layers, src, stiff, buoy, pressure, velocity, load_in, flux_in, up, down):
    everywhere = tuple(range(layers))
    above, under = layers, layers + 1
    pa = xa = ya = za = pa2 = None
    pb = xb = yb = zb = pb2 = xb2 = None
    for k in range(steps):
        inner = 0 < k < steps - 1
        load = []
        for i in everywhere:
            p = src(k, i) if k == 0 else pressure[i] + src(k, i)
            pressure[i] = p
            load.append(stiff(i) * p)
        beyond = load_in(k)
        if k > 0:
            la = up[0] * pa
            beyond = beyond + la
            lb = down[0] * pb
        if inner:
            xa = -la if xa is None else xa - la
            if pa2 is not None:
                xa = xa + up[1] * pa2
            y, z = space.fwd_y(la), space.fwd_z(la, load_key(k, above))
            ya, za = (y, z) if ya is None else (ya + y, za + z)
            y, z = space.fwd_y(lb), space.fwd_z(lb, load_key(k, under))
            yb, zb = (y, z) if yb is None else (yb + y, zb + z)
            xb2 = lb if xb2 is None else xb2 + lb
            if pb2 is not None:
                xb2 = xb2 - down[1] * pb2
        xb = load[0] if k == 0 else xb + load[0] - lb
        fb = down[2] * xb
        below = flux_in(k) + fb
        for i in everywhere:
            x = (load[i + 1] if i + 1 < layers else beyond) - load[i]
            y = space.fwd_y(load[i])
            z = space.fwd_z(load[i], load_key(k, i))
            if k > 0:
                x, y, z = velocity[0, i] + x, velocity[1, i] + y, velocity[2, i] + z
            velocity[0, i], velocity[1, i], velocity[2, i] = x, y, z
            fx = buoy(i) * x
            spread = fx - below
            spread = spread + space.bwd_y(buoy(i) * y)
            spread = spread + space.bwd_z(buoy(i) * z, flux_key(k, i))
            pressure[i] = pressure[i] + spread
            below = fx
        if k == steps - 1:
            return
        if k == 0:
            pa, pb = -below, fb
            continue
        fa = up[2] * xa
        pa = pa + fa - below
        pa = pa + space.bwd_y(up[2] * ya) + space.bwd_z(up[2] * za, flux_key(k, above))
        fb2 = down[3] * xb2
        pb = pb + fb - fb2
        pb = pb + space.bwd_y(down[2] * yb) + space.bwd_z(down[2] * zb, flux_key(k, under))
        if k < steps - 2:
            pa2, pb2 = -fa, fb2


class Layers:
    def __init__(self, ref):
        self.ref = ref

    def __getitem__(self, i):
        return self.ref[i]

    def __setitem__(self, i, value):
        self.ref[i] = value


def pack_kernel(steps, layers, src, speed, imped, low, high, own):
    lanes = src.shape[-1]
    rows = layers * EDGE
    row, lane = iota((rows, lanes), 0), iota((rows, lanes), 1)
    wrow, wlane = iota((WIDE, lanes), 0), iota((WIDE, lanes), 1)
    half = WIDE // 2
    at_low = (wrow >= EDGE) & (wrow < half) & (wlane == wrow - EDGE)
    at_high = (wrow >= half) & (wrow < half + OWN) & (wlane == wrow + (lanes - OWN - half))
    wide = jnp.where(at_low | at_high, 1.0, 0.0)
    for f in range(steps + 2):
        total = None
        for i in range(layers):
            mine = (row >> 2) == i
            picks = [mine & (lane == base + (row & 3)) for base in (0, lanes - EDGE)]
            pick = jnp.concatenate([wide] + [jnp.where(p, 1.0, 0.0) for p in picks], 0).astype(jnp.bfloat16)
            if f < steps:
                block = brick_block(src, f, i).astype(jnp.bfloat16)
            else:
                block = (speed, imped)[f - steps][i]
            part = lax.dot_general(pick, block, (((1,), (1,)), ((), ())), preferred_element_type=jnp.float32)
            own[f, i * WIDE : (i + 1) * WIDE, :] = part[:WIDE]
            total = part[WIDE:] if total is None else total + part[WIDE:]
        low[f * rows : (f + 1) * rows, :] = total[:rows].astype(jnp.bfloat16)
        high[f * rows : (f + 1) * rows, :] = total[rows:].astype(jnp.bfloat16)


def strip_rows(message, at, lanes):
    parts = [f32(message[at + j * STRIP : at + (j + 1) * STRIP, :]) for j in range(lanes // 128)]
    return parts[0] if len(parts) == 1 else jnp.concatenate(parts, 1)


def put_strip(message, at, strip):
    for j in range(strip.shape[1] // 128):
        message[at + j * STRIP : at + (j + 1) * STRIP, :] = strip[:, j * 128 : (j + 1) * 128].astype(jnp.bfloat16)


def is_even():
    return lax.axis_index("gx") % 2 == 0


class Faces:
    def __init__(self, far, near):
        self.far, self.near = far, near
        self.even = is_even()

    def put(self, write, below, above):
        write(self.far, jnp.where(self.even, below, above))
        write(self.near, jnp.where(self.even, above, below))

    def above(self, read):
        return jnp.where(self.even, read(self.near), read(self.far))

    def below(self, read):
        return jnp.where(self.even, read(self.far), read(self.near))


class Series:
    def __init__(self, faces, write):
        self.faces, self.write, self.loads = faces, write, {}

    def put_load(self, k, a):
        self.loads[k] = a

    def put_flux(self, k, a):
        self.faces.put(lambda ref, value: self.write(ref, k, value), self.loads[k], a)


def rows_writer(rows):
    def write(ref, k, a):
        ref[k * rows : (k + 1) * rows, :] = a.astype(jnp.bfloat16)
    return write


def rows_reader(rows):
    return lambda k: lambda ref: f32(ref[k * rows : (k + 1) * rows, :])


def strip_layout(steps, y):
    step = STRIP * (y // 128)
    return step, steps * step


def coefficients_kernel(speed, imped, stiff, buoy):
    for i in range(speed.shape[0]):
        stiff[i], buoy[i] = coefficients(f32(speed[i]), f32(imped[i]))


def cut_kernel(steps, layers, src, stiff, buoy, far, near, pressure, velocity):
    y, lanes = stiff.shape[1:]
    out = Series(Faces(far, near), rows_writer(y))
    run_cut(
        Block((y, lanes), None), steps, layers, lambda k, i: brick_block(src, steps - 1 - k, i),
        lambda i: stiff[i], lambda i: buoy[i], Layers(pressure), Layers(velocity), out.put_load, out.put_flux,
    )


def edge_kernel(steps, layers, gy_size, own, left, right, far, near, strips, whole):
    y = own.shape[2]
    rows = layers * EDGE
    me = lax.axis_index("gy")
    shape = (layers * WIDE, 2 * rows)
    r, c = iota(shape, 0), iota(shape, 1)
    inside = r & (WIDE - 1)
    at = (r >> 5) * EDGE + (r & 3)
    wanted = (inside < EDGE) & (c == at) & (me > 0)
    wanted = wanted | ((inside >= WIDE - EDGE) & (c == rows + at) & (me < gy_size - 1))
    order = jnp.where(wanted, 1.0, 0.0).astype(jnp.bfloat16)

    def narrow(a):
        half = STRIP // 2
        return jnp.concatenate([a[:half], a[WIDE - half :]], 0)

    for f in range(steps + 2):
        parts = jnp.concatenate([a[f * rows : (f + 1) * rows, :] for a in (left, right)], 0)
        whole[f] = own[f] + jnp.dot(order, parts, preferred_element_type=jnp.float32)
        for i in range(layers):
            strips[f, i * STRIP : (i + 1) * STRIP, :] = narrow(whole[f, i * WIDE : (i + 1) * WIDE, :])

    def strip(f, i):
        return whole[f, i * WIDE : (i + 1) * WIDE, :]

    faces = Faces(far, near)
    step, extra = strip_layout(steps, y)
    last = layers - 1
    for j, (f, depth) in enumerate(((steps, 0), (steps, 1), (steps + 1, 0), (steps + 1, 1))):
        faces.put(
            lambda ref, value, at=extra + j * step: put_strip(ref, at, value),
            narrow(strip(f, depth)), narrow(strip(f, last - depth)),
        )
    coef = [coefficients(strip(steps, i), strip(steps + 1, i)) for i in range(layers)]
    out = Series(faces, lambda ref, k, a: put_strip(ref, k * step, narrow(a)))
    run_cut(
        Strip((WIDE, y), None), steps, layers, lambda k, i: strip(steps - 1 - k, i),
        lambda i: coef[i][0], lambda i: coef[i][1], {}, {}, out.put_load, out.put_flux,
    )


def outer_key(step, side):
    return 64 + ((step - 1) * 2 + side) * 8


def joined_kernel(
    steps, layers, src, stiff, buoy, strips, far, near, edge_far, edge_near, coef_far, coef_near,
    pressure, velocity, series, columns,
):
    y, lanes = stiff.shape[1:]

    def strip(f, i):
        return strips[f, i * STRIP : (i + 1) * STRIP, :]

    faces = Faces(edge_far, edge_near)
    step, extra = strip_layout(steps, y)
    outer = EDGE - 1
    series[...] = jnp.zeros(series.shape, jnp.float32)

    def strip_at(at):
        return lambda ref: strip_rows(ref, at, y)

    def edge_face(side):
        def read(k):
            a = (faces.above, faces.below)[side](strip_at(k * step))
            if k > 0:
                at = outer_key(k, side)
                series[at : at + outer, :] = a[HIGH - outer : HIGH, :]
                series[at + outer : at + 2 * outer, :] = a[LOW + 1 : LOW + 1 + outer, :]
            return a
        return read

    def beside(side, at):
        s = [side(at(j)) for j in range(4)]
        (stiff, buoy), (stiff2, buoy2) = coefficients(s[0], s[2]), coefficients(s[1], s[3])
        return stiff, stiff2, buoy, buoy2

    coef = [coefficients(strip(steps, i), strip(steps + 1, i)) for i in range(layers)]
    run_joined(
        Strip((STRIP, y), series), steps, layers, lambda k, i: strip(steps - 1 - k, i),
        lambda i: coef[i][0], lambda i: coef[i][1], {}, {}, edge_face(0), edge_face(1),
        beside(faces.above, lambda j: strip_at(extra + j * step)),
        beside(faces.below, lambda j: strip_at(extra + j * step)),
    )
    columns[...] = series[...].T

    held = Faces(coef_far, coef_near)
    main = Faces(far, near)
    read = rows_reader(y)
    lane = iota((y, lanes), 1)

    def face(side):
        def get(k):
            a = (main.above, main.below)[side](read(k))
            if k == 0:
                return a
            placed = pltpu.roll(columns[...], (lanes - outer - outer_key(k, side)) % lanes, 1)
            return jnp.where((lane < k) | (lane >= lanes - k), placed, a)
        return get

    run_joined(
        Block((y, lanes), columns), steps, layers, lambda k, i: brick_block(src, steps - 1 - k, i),
        lambda i: stiff[i], lambda i: buoy[i], Layers(pressure), Layers(velocity), face(0), face(1),
        beside(held.above, lambda j: lambda ref: f32(ref[j])),
        beside(held.below, lambda j: lambda ref: f32(ref[j])),
    )


def shifted(block, axis, distance):
    devices = range(lax.axis_size(axis))
    return lax.ppermute(block, axis, [(i, i + distance) for i in devices if i + distance in devices])


def swapped(block, axis, first):
    pairs = [(i, i + 1) for i in range(first, lax.axis_size(axis) - 1, 2)]
    return lax.ppermute(block, axis, pairs + [(j, i) for i, j in pairs])


def on_device(source, speed, impedance):
    steps, whole_x, brick_y, lanes = source.shape
    layers, y, _ = speed.shape
    assert layers == steps == EDGE and lanes == 128 and y % 128 == 0
    gy_size = lax.axis_size("gy")
    xs = ("grp", "gx")
    bf16 = jnp.bfloat16
    params = pltpu.CompilerParams(vmem_limit_bytes=32 * 1024 * 1024)
    sds = jax.ShapeDtypeStruct

    assert lax.axis_size("gx") % 2 == 0
    below = jnp.concatenate([speed[:2], impedance[:2]], 0)
    above = jnp.concatenate([speed[-1:], speed[-2:-1], impedance[-1:], impedance[-2:-1]], 0)
    even = is_even()
    coef_far, coef_near = jnp.where(even, below, above), jnp.where(even, above, below)
    coef_far, coef_near = swapped(coef_far, xs, 1), swapped(coef_near, xs, 0)
    relaid = lax.all_to_all(source.transpose(1, 0, 2, 3), xs, split_axis=0, concat_axis=0, tiled=True)
    relaid = relaid.reshape(whole_x // layers, layers, steps, brick_y, lanes)
    field = sds((layers, y, lanes), jnp.float32)
    stiff, buoy = pl.pallas_call(
        coefficients_kernel, out_shape=(field, field), compiler_params=params, name="coefficients"
    )(speed, impedance)
    relaid, coef_far, coef_near, stiff, buoy = lax.optimization_barrier((relaid, coef_far, coef_near, stiff, buoy))

    def call(kernel, outs, scratch, *args, name):
        return pl.pallas_call(kernel, out_shape=outs, scratch_shapes=scratch, compiler_params=params, name=name)(*args)

    edge = sds(((steps + 2) * layers * EDGE, y), bf16)
    low, high, own = call(
        functools.partial(pack_kernel, steps, layers),
        (edge, edge, sds((steps + 2, layers * WIDE, y), jnp.float32)), [], relaid, speed, impedance, name="pack",
    )
    if gy_size == 2:
        left = right = lax.ppermute(jnp.where(lax.axis_index("gy") == 0, high, low), "gy", [(0, 1), (1, 0)])
    else:
        left, right = shifted(high, "gy", 1), shifted(low, "gy", -1)

    message = sds((steps * y, 128), bf16)
    far, near = call(
        functools.partial(cut_kernel, steps, layers), (message, message),
        [pltpu.VMEM((layers, y, lanes), jnp.float32), pltpu.VMEM((3, layers, y, lanes), jnp.float32)],
        relaid, stiff, buoy, name="cut",
    )
    far, near, left, right = lax.optimization_barrier((far, near, left, right))
    far, near = swapped(far, xs, 1), swapped(near, xs, 0)

    message = sds(((steps + 4) * STRIP * (y // 128), 128), bf16)
    edge_far, edge_near, strips = call(
        functools.partial(edge_kernel, steps, layers, gy_size),
        (message, message, sds((steps + 2, layers * STRIP, y), jnp.float32)),
        [pltpu.VMEM((steps + 2, layers * WIDE, y), jnp.float32)], own, left, right, name="edge",
    )
    edge_far, edge_near = swapped(edge_far, xs, 1), swapped(edge_near, xs, 0)

    return call(
        functools.partial(joined_kernel, steps, layers), (field, sds((3, layers, y, lanes), jnp.float32)),
        [pltpu.VMEM((128, y), jnp.float32), pltpu.VMEM((y, 128), jnp.float32)],
        relaid, stiff, buoy, strips, far, near, edge_far, edge_near, coef_far, coef_near, name="joined",
    )


def solution(mesh):
    in_specs = (
        P(None, None, ("grp", "gx"), "gy"),
        P(("grp", "gx"), None, "gy"),
        P(("grp", "gx"), None, "gy"),
    )
    out_specs = (P(("grp", "gx"), None, "gy"), P(None, ("grp", "gx"), None, "gy"))
    return jax.shard_map(
        on_device, mesh=mesh, in_specs=in_specs, out_specs=out_specs, check_vma=False
    )
```

```python
import functools

import jax
import jax.numpy as jnp
from jax import lax
from jax.experimental import pallas as pl
from jax.experimental.pallas import tpu as pltpu
from jax.sharding import PartitionSpec as P

courant = 0.15
EDGE = 4
STRIP = 4 * EDGE
OWN = 3 * EDGE
WIDE = 2 * (OWN + EDGE)
LOW, HIGH = EDGE - 1, 3 * EDGE


def f32(x):
    return x.astype(jnp.float32)


def iota(shape, dim):
    return lax.broadcasted_iota(jnp.int32, shape, dim)


def brick_block(src, step, layer):
    bricks = f32(src[:, layer, step])
    return bricks.reshape(bricks.shape[0] * bricks.shape[1], bricks.shape[2])


def coefficients(speed, imped):
    held = imped > 0.0
    stiff = courant * (speed * imped)
    buoy = jnp.where(held, courant * (speed / jnp.where(held, imped, 1.0)), 0.0)
    return stiff, buoy


class Block:
    def __init__(self, shape, series):
        self.row, self.lane = iota(shape, 0), iota(shape, 1)
        self.rows, self.lanes = shape
        self.series = series

    def fwd_y(self, a):
        return jnp.where(self.row == self.rows - 1, 0.0, pltpu.roll(a, self.rows - 1, 0)) - a

    def bwd_y(self, g):
        return g - jnp.where(self.row == 0, 0.0, pltpu.roll(g, 1, 0))

    def column(self, key):
        return 0.0 if self.series is None else self.series[:, key : key + 1]

    def fwd_z(self, a, key):
        col = self.column(key)
        return jnp.where(self.lane == self.lanes - 1, col, pltpu.roll(a, self.lanes - 1, 1)) - a

    def bwd_z(self, g, key):
        col = self.column(key)
        return g - jnp.where(self.lane == 0, col, pltpu.roll(g, 1, 1))


class Strip:
    def __init__(self, shape, series):
        self.lane = iota(shape, 1)
        self.rows, self.lanes = shape
        self.series = series

    def fwd_y(self, a):
        return jnp.where(self.lane == self.lanes - 1, 0.0, pltpu.roll(a, self.lanes - 1, 1)) - a

    def bwd_y(self, g):
        return g - jnp.where(self.lane == 0, 0.0, pltpu.roll(g, 1, 1))

    def fwd_z(self, a, key):
        if self.series is not None:
            self.series[key : key + 1, :] = a[HIGH : HIGH + 1, :]
        return pltpu.roll(a, self.rows - 1, 0) - a

    def bwd_z(self, g, key):
        if self.series is not None:
            self.series[key : key + 1, :] = g[LOW : LOW + 1, :]
        return g - pltpu.roll(g, 1, 0)


def load_key(step, layer):
    return step * 16 + layer


def flux_key(step, layer):
    return step * 16 + 8 + layer


def run_cut(space, steps, layers, src, stiff, buoy, pressure, velocity, put_load, put_flux):
    ends = (0, layers - 1)
    everywhere = tuple(range(layers))
    for k in range(steps):
        load = []
        for i in everywhere if k < steps - 1 else ends:
            p = src(k, i) if k == 0 else pressure[i] + src(k, i)
            pressure[i] = p
            load.append(stiff(i) * p)
        put_load(k, load[0])
        if k == steps - 1:
            put_flux(k, buoy(layers - 1) * (velocity[0, layers - 1] - load[-1]))
            return
        wanted = everywhere if k < steps - 2 else ends
        below = None
        for i in everywhere:
            x = (load[i + 1] - load[i]) if i + 1 < layers else -load[i]
            if k > 0:
                x = velocity[0, i] + x
            velocity[0, i] = x
            fx = buoy(i) * x
            if i == layers - 1:
                put_flux(k, fx)
            if i in wanted:
                y = space.fwd_y(load[i])
                z = space.fwd_z(load[i], load_key(k, i))
                if k > 0:
                    y, z = velocity[1, i] + y, velocity[2, i] + z
                velocity[1, i], velocity[2, i] = y, z
                spread = fx if i == 0 else fx - below
                spread = spread + space.bwd_y(buoy(i) * y)
                spread = spread + space.bwd_z(buoy(i) * z, flux_key(k, i))
                pressure[i] = pressure[i] + spread
            below = fx


def run_joined(space, steps, layers, src, stiff, buoy, pressure, velocity, load_in, flux_in, up, down, finished=None):
    everywhere = tuple(range(layers))
    above, under = layers, layers + 1
    pa = xa = ya = za = pa2 = None
    pb = xb = yb = zb = pb2 = xb2 = None
    for k in range(steps):
        inner = 0 < k < steps - 1
        load = []
        for i in everywhere:
            p = src(k, i) if k == 0 else pressure[i] + src(k, i)
            pressure[i] = p
            load.append(stiff(i) * p)
        beyond = load_in(k)
        if k > 0:
            la = up[0] * pa
            beyond = beyond + la
            lb = down[0] * pb
        if inner:
            xa = -la if xa is None else xa - la
            if pa2 is not None:
                xa = xa + up[1] * pa2
            y, z = space.fwd_y(la), space.fwd_z(la, load_key(k, above))
            ya, za = (y, z) if ya is None else (ya + y, za + z)
            y, z = space.fwd_y(lb), space.fwd_z(lb, load_key(k, under))
            yb, zb = (y, z) if yb is None else (yb + y, zb + z)
            xb2 = lb if xb2 is None else xb2 + lb
            if pb2 is not None:
                xb2 = xb2 - down[1] * pb2
        xb = load[0] if k == 0 else xb + load[0] - lb
        fb = down[2] * xb
        below = flux_in(k) + fb
        for i in everywhere:
            x = (load[i + 1] if i + 1 < layers else beyond) - load[i]
            y = space.fwd_y(load[i])
            z = space.fwd_z(load[i], load_key(k, i))
            if k > 0:
                x, y, z = velocity[0, i] + x, velocity[1, i] + y, velocity[2, i] + z
            velocity[0, i], velocity[1, i], velocity[2, i] = x, y, z
            fx = buoy(i) * x
            spread = fx - below
            spread = spread + space.bwd_y(buoy(i) * y)
            spread = spread + space.bwd_z(buoy(i) * z, flux_key(k, i))
            pressure[i] = pressure[i] + spread
            below = fx
            if k == steps - 1 and finished is not None:
                finished(i)
        if k == steps - 1:
            return
        if k == 0:
            pa, pb = -below, fb
            continue
        fa = up[2] * xa
        pa = pa + fa - below
        pa = pa + space.bwd_y(up[2] * ya) + space.bwd_z(up[2] * za, flux_key(k, above))
        fb2 = down[3] * xb2
        pb = pb + fb - fb2
        pb = pb + space.bwd_y(down[2] * yb) + space.bwd_z(down[2] * zb, flux_key(k, under))
        if k < steps - 2:
            pa2, pb2 = -fa, fb2


class Layers:
    def __init__(self, ref):
        self.ref = ref

    def __getitem__(self, i):
        return self.ref[i]

    def __setitem__(self, i, value):
        self.ref[i] = value


def pack_kernel(steps, layers, src, speed, imped, low, high, own):
    lanes = src.shape[-1]
    rows = layers * EDGE
    row, lane = iota((rows, lanes), 0), iota((rows, lanes), 1)
    wrow, wlane = iota((WIDE, lanes), 0), iota((WIDE, lanes), 1)
    half = WIDE // 2
    at_low = (wrow >= EDGE) & (wrow < half) & (wlane == wrow - EDGE)
    at_high = (wrow >= half) & (wrow < half + OWN) & (wlane == wrow + (lanes - OWN - half))
    wide = jnp.where(at_low | at_high, 1.0, 0.0)
    for f in range(steps + 2):
        total = None
        for i in range(layers):
            mine = (row >> 2) == i
            picks = [mine & (lane == base + (row & 3)) for base in (0, lanes - EDGE)]
            pick = jnp.concatenate([wide] + [jnp.where(p, 1.0, 0.0) for p in picks], 0).astype(jnp.bfloat16)
            if f < steps:
                block = brick_block(src, f, i).astype(jnp.bfloat16)
            else:
                block = (speed, imped)[f - steps][i]
            part = lax.dot_general(pick, block, (((1,), (1,)), ((), ())), preferred_element_type=jnp.float32)
            own[f, i * WIDE : (i + 1) * WIDE, :] = part[:WIDE]
            total = part[WIDE:] if total is None else total + part[WIDE:]
        low[f * rows : (f + 1) * rows, :] = total[:rows].astype(jnp.bfloat16)
        high[f * rows : (f + 1) * rows, :] = total[rows:].astype(jnp.bfloat16)


def strip_rows(message, at, lanes):
    parts = [f32(message[at + j * STRIP : at + (j + 1) * STRIP, :]) for j in range(lanes // 128)]
    return parts[0] if len(parts) == 1 else jnp.concatenate(parts, 1)


def put_strip(message, at, strip):
    for j in range(strip.shape[1] // 128):
        message[at + j * STRIP : at + (j + 1) * STRIP, :] = strip[:, j * 128 : (j + 1) * 128].astype(jnp.bfloat16)


def is_even():
    return lax.axis_index("gx") % 2 == 0


class Faces:
    def __init__(self, far, near):
        self.far, self.near = far, near
        self.even = is_even()

    def put(self, write, below, above):
        write(self.far, jnp.where(self.even, below, above))
        write(self.near, jnp.where(self.even, above, below))

    def above(self, read):
        return jnp.where(self.even, read(self.near), read(self.far))

    def below(self, read):
        return jnp.where(self.even, read(self.far), read(self.near))


def rows_writer(rows):
    def write(ref, k, a):
        ref[k * rows : (k + 1) * rows, :] = a.astype(jnp.bfloat16)
    return write


def rows_reader(rows):
    return lambda k: lambda ref: f32(ref[k * rows : (k + 1) * rows, :])


def strip_layout(steps, y):
    step = STRIP * (y // 128)
    return step, steps * y, steps * y + steps * step


def bricks_kernel(source, bricks):
    for k in range(source.shape[0]):
        bricks[:, k] = source[k]


def coefficients_kernel(speed, imped, stiff, buoy):
    for i in range(speed.shape[0]):
        stiff[i], buoy[i] = coefficients(f32(speed[i]), f32(imped[i]))


def cut_kernel(steps, layers, src, stiff, buoy, loads, fluxes, pressure, velocity):
    y, lanes = stiff.shape[1:]
    write = rows_writer(y)
    run_cut(
        Block((y, lanes), None), steps, layers, lambda k, i: brick_block(src, steps - 1 - k, i),
        lambda i: stiff[i], lambda i: buoy[i], Layers(pressure), Layers(velocity),
        lambda k, a: write(loads, k, a), lambda k, a: write(fluxes, k, a),
    )


def edge_kernel(
    steps, layers, gy_size, own, left, right, loads, fluxes, far, near, strips, whole, series, columns
):
    y, lanes = own.shape[2], loads.shape[1]
    rows = layers * EDGE
    me = lax.axis_index("gy")
    shape = (layers * WIDE, 2 * rows)
    r, c = iota(shape, 0), iota(shape, 1)
    inside = r & (WIDE - 1)
    at = (r >> 5) * EDGE + (r & 3)
    wanted = (inside < EDGE) & (c == at) & (me > 0)
    wanted = wanted | ((inside >= WIDE - EDGE) & (c == rows + at) & (me < gy_size - 1))
    order = jnp.where(wanted, 1.0, 0.0).astype(jnp.bfloat16)

    def narrow(a):
        half = STRIP // 2
        return jnp.concatenate([a[:half], a[WIDE - half :]], 0)

    for f in range(steps + 2):
        parts = jnp.concatenate([a[f * rows : (f + 1) * rows, :] for a in (left, right)], 0)
        whole[f] = own[f] + jnp.dot(order, parts, preferred_element_type=jnp.float32)
        for i in range(layers):
            strips[f, i * STRIP : (i + 1) * STRIP, :] = narrow(whole[f, i * WIDE : (i + 1) * WIDE, :])

    def strip(f, i):
        return whole[f, i * WIDE : (i + 1) * WIDE, :]

    faces = Faces(far, near)
    step, base, extra = strip_layout(steps, y)
    last = layers - 1
    for j, (f, depth) in enumerate(((steps, 0), (steps, 1), (steps + 1, 0), (steps + 1, 1))):
        faces.put(
            lambda ref, value, at=extra + j * step: put_strip(ref, at, value),
            narrow(strip(f, depth)), narrow(strip(f, last - depth)),
        )
    coef = [coefficients(strip(steps, i), strip(steps + 1, i)) for i in range(layers)]
    strip_loads, strip_fluxes = {}, {}
    run_cut(
        Strip((WIDE, y), None), steps, layers, lambda k, i: strip(steps - 1 - k, i),
        lambda i: coef[i][0], lambda i: coef[i][1], {}, {}, strip_loads.__setitem__, strip_fluxes.__setitem__,
    )
    outer = EDGE - 1
    series[...] = jnp.zeros(series.shape, jnp.float32)
    for k in range(steps):
        pair = narrow(strip_loads[k]), narrow(strip_fluxes[k])
        faces.put(lambda ref, value: put_strip(ref, base + k * step, value), *pair)
        if k > 0:
            for side, a in enumerate(pair):
                at = outer_key(k, side)
                series[at : at + outer, :] = a[HIGH - outer : HIGH, :]
                series[at + outer : at + 2 * outer, :] = a[LOW + 1 : LOW + 1 + outer, :]
    columns[...] = series[...].T

    lane = iota((y, lanes), 1)
    read, write = rows_reader(y), rows_writer(y)

    def merged(ref, k, side):
        a = read(k)(ref)
        if k == 0:
            return a
        placed = pltpu.roll(columns[...], (lanes - outer - outer_key(k, side)) % lanes, 1)
        return jnp.where((lane < k) | (lane >= lanes - k), placed, a)

    for k in range(steps):
        faces.put(lambda ref, value: write(ref, k, value), merged(loads, k, 0), merged(fluxes, k, 1))


def outer_key(step, side):
    return ((step - 1) * 2 + side) * 8


def joined_kernel(
    steps, layers, src, stiff, buoy, strips, far, near, coef_far, coef_near, pressure_out, velocity_out,
    pressure, velocity, series, columns, sems,
):
    y, lanes = stiff.shape[1:]

    def strip(f, i):
        return strips[f, i * STRIP : (i + 1) * STRIP, :]

    faces = Faces(far, near)
    step, base, extra = strip_layout(steps, y)

    def strip_at(at):
        return lambda ref: strip_rows(ref, at, y)

    def beside(side, at):
        s = [side(at(j)) for j in range(4)]
        (stiff, buoy), (stiff2, buoy2) = coefficients(s[0], s[2]), coefficients(s[1], s[3])
        return stiff, stiff2, buoy, buoy2

    coef = [coefficients(strip(steps, i), strip(steps + 1, i)) for i in range(layers)]
    series[...] = jnp.zeros(series.shape, jnp.float32)
    run_joined(
        Strip((STRIP, y), series), steps, layers, lambda k, i: strip(steps - 1 - k, i),
        lambda i: coef[i][0], lambda i: coef[i][1], {}, {},
        lambda k: faces.above(strip_at(base + k * step)), lambda k: faces.below(strip_at(base + k * step)),
        beside(faces.above, lambda j: strip_at(extra + j * step)),
        beside(faces.below, lambda j: strip_at(extra + j * step)),
    )
    columns[...] = series[...].T

    def copies(i):
        return (
            pltpu.make_async_copy(velocity.at[:, i], velocity_out.at[:, i], sems.at[0, i]),
            pltpu.make_async_copy(pressure.at[i], pressure_out.at[i], sems.at[1, i]),
        )

    def send(i):
        for copy in copies(i):
            copy.start()

    held = Faces(coef_far, coef_near)
    read = rows_reader(y)
    run_joined(
        Block((y, lanes), columns), steps, layers, lambda k, i: brick_block(src, steps - 1 - k, i),
        lambda i: stiff[i], lambda i: buoy[i], Layers(pressure), Layers(velocity),
        lambda k: faces.above(read(k)), lambda k: faces.below(read(k)),
        beside(held.above, lambda j: lambda ref: f32(ref[j])),
        beside(held.below, lambda j: lambda ref: f32(ref[j])),
        send,
    )
    for i in range(layers):
        for copy in copies(i):
            copy.wait()


def shifted(block, axis, distance):
    devices = range(lax.axis_size(axis))
    return lax.ppermute(block, axis, [(i, i + distance) for i in devices if i + distance in devices])


def swapped(block, axis, first):
    pairs = [(i, i + 1) for i in range(first, lax.axis_size(axis) - 1, 2)]
    return lax.ppermute(block, axis, pairs + [(j, i) for i, j in pairs])


def on_device(source, speed, impedance):
    steps, whole_x, brick_y, lanes = source.shape
    layers, y, _ = speed.shape
    assert layers == steps == EDGE and lanes == 128 and y % 128 == 0
    gy_size = lax.axis_size("gy")
    xs = ("grp", "gx")
    bf16 = jnp.bfloat16
    params = pltpu.CompilerParams(vmem_limit_bytes=32 * 1024 * 1024)
    sds = jax.ShapeDtypeStruct

    assert lax.axis_size("gx") % 2 == 0
    below = jnp.concatenate([speed[:2], impedance[:2]], 0)
    above = jnp.concatenate([speed[-1:], speed[-2:-1], impedance[-1:], impedance[-2:-1]], 0)
    even = is_even()
    coef_far, coef_near = jnp.where(even, below, above), jnp.where(even, above, below)
    coef_far, coef_near = swapped(coef_far, xs, 1), swapped(coef_near, xs, 0)
    chunk = whole_x // 4
    bricks = pl.pallas_call(
        bricks_kernel,
        grid=(4,),
        in_specs=[pl.BlockSpec((steps, chunk, brick_y, lanes), lambda j: (0, j, 0, 0))],
        out_specs=pl.BlockSpec((chunk, steps, brick_y, lanes), lambda j: (j, 0, 0, 0)),
        out_shape=sds((whole_x, steps, brick_y, lanes), bf16),
        compiler_params=pltpu.CompilerParams(vmem_limit_bytes=60 * 1024 * 1024),
        name="bricks",
    )(source)
    relaid = lax.all_to_all(bricks, xs, split_axis=0, concat_axis=0, tiled=True)
    relaid = relaid.reshape(whole_x // layers, layers, steps, brick_y, lanes)
    field = sds((layers, y, lanes), jnp.float32)
    stiff, buoy = pl.pallas_call(
        coefficients_kernel, out_shape=(field, field), compiler_params=params, name="coefficients"
    )(speed, impedance)
    relaid, coef_far, coef_near, stiff, buoy = lax.optimization_barrier((relaid, coef_far, coef_near, stiff, buoy))

    def call(kernel, outs, scratch, *args, name):
        return pl.pallas_call(kernel, out_shape=outs, scratch_shapes=scratch, compiler_params=params, name=name)(*args)

    edge = sds(((steps + 2) * layers * EDGE, y), bf16)
    low, high, own = call(
        functools.partial(pack_kernel, steps, layers),
        (edge, edge, sds((steps + 2, layers * WIDE, y), jnp.float32)), [], relaid, speed, impedance, name="pack",
    )
    if gy_size == 2:
        left = right = lax.ppermute(jnp.where(lax.axis_index("gy") == 0, high, low), "gy", [(0, 1), (1, 0)])
    else:
        left, right = shifted(high, "gy", 1), shifted(low, "gy", -1)

    whole = pltpu.VMEM((layers, y, lanes), jnp.float32)
    whole_velocity = pltpu.VMEM((3, layers, y, lanes), jnp.float32)
    series = [pltpu.VMEM((128, y), jnp.float32), pltpu.VMEM((y, 128), jnp.float32)]
    face = sds((steps * y, 128), bf16)
    loads, fluxes = call(
        functools.partial(cut_kernel, steps, layers), (face, face), [whole, whole_velocity], relaid, stiff, buoy, name="cut"
    )
    _, _, extra = strip_layout(steps, y)
    message = sds((extra + 4 * STRIP * (y // 128), 128), bf16)
    far, near, strips = call(
        functools.partial(edge_kernel, steps, layers, gy_size),
        (message, message, sds((steps + 2, layers * STRIP, y), jnp.float32)),
        [pltpu.VMEM((steps + 2, layers * WIDE, y), jnp.float32)] + series,
        own, left, right, loads, fluxes, name="edge",
    )
    far, near = swapped(far, xs, 1), swapped(near, xs, 0)

    args = relaid, stiff, buoy, strips, far, near, coef_far, coef_near
    return pl.pallas_call(
        functools.partial(joined_kernel, steps, layers),
        in_specs=[pl.BlockSpec(memory_space=pltpu.VMEM)] * len(args),
        out_specs=(pl.BlockSpec(memory_space=pl.ANY), pl.BlockSpec(memory_space=pl.ANY)),
        out_shape=(field, sds((3, layers, y, lanes), jnp.float32)),
        scratch_shapes=[whole, whole_velocity] + series + [pltpu.SemaphoreType.DMA((2, layers))],
        compiler_params=params,
        name="joined",
    )(*args)


def solution(mesh):
    in_specs = (
        P(None, None, ("grp", "gx"), "gy"),
        P(("grp", "gx"), None, "gy"),
        P(("grp", "gx"), None, "gy"),
    )
    out_specs = (P(("grp", "gx"), None, "gy"), P(None, ("grp", "gx"), None, "gy"))
    return jax.shard_map(
        on_device, mesh=mesh, in_specs=in_specs, out_specs=out_specs, check_vma=False
    )
```

```python
import functools

import jax
import jax.numpy as jnp
from jax import lax
from jax.experimental import pallas as pl
from jax.experimental.pallas import tpu as pltpu
from jax.sharding import PartitionSpec as P

courant = 0.15
EDGE = 4
STRIP = 4 * EDGE
OWN = 3 * EDGE
WIDE = 2 * (OWN + EDGE)
LOW, HIGH = EDGE - 1, 3 * EDGE


def f32(x):
    return x.astype(jnp.float32)


def iota(shape, dim):
    return lax.broadcasted_iota(jnp.int32, shape, dim)


def brick_block(src, step, layer):
    bricks = f32(src[:, layer, step])
    return bricks.reshape(bricks.shape[0] * bricks.shape[1], bricks.shape[2])


def coefficients(speed, imped):
    held = imped > 0.0
    stiff = courant * (speed * imped)
    buoy = jnp.where(held, courant * (speed / jnp.where(held, imped, 1.0)), 0.0)
    return stiff, buoy


class Block:
    def __init__(self, shape, series):
        self.row, self.lane = iota(shape, 0), iota(shape, 1)
        self.rows, self.lanes = shape
        self.series = series

    def fwd_y(self, a):
        return jnp.where(self.row == self.rows - 1, 0.0, pltpu.roll(a, self.rows - 1, 0)) - a

    def bwd_y(self, g):
        return g - jnp.where(self.row == 0, 0.0, pltpu.roll(g, 1, 0))

    def column(self, key):
        return 0.0 if self.series is None else self.series[:, key : key + 1]

    def fwd_z(self, a, key):
        col = self.column(key)
        return jnp.where(self.lane == self.lanes - 1, col, pltpu.roll(a, self.lanes - 1, 1)) - a

    def bwd_z(self, g, key):
        col = self.column(key)
        return g - jnp.where(self.lane == 0, col, pltpu.roll(g, 1, 1))


class Strip:
    def __init__(self, shape, series):
        self.lane = iota(shape, 1)
        self.rows, self.lanes = shape
        self.series = series

    def fwd_y(self, a):
        return jnp.where(self.lane == self.lanes - 1, 0.0, pltpu.roll(a, self.lanes - 1, 1)) - a

    def bwd_y(self, g):
        return g - jnp.where(self.lane == 0, 0.0, pltpu.roll(g, 1, 1))

    def fwd_z(self, a, key):
        if self.series is not None:
            self.series[key : key + 1, :] = a[HIGH : HIGH + 1, :]
        return pltpu.roll(a, self.rows - 1, 0) - a

    def bwd_z(self, g, key):
        if self.series is not None:
            self.series[key : key + 1, :] = g[LOW : LOW + 1, :]
        return g - pltpu.roll(g, 1, 0)


def load_key(step, layer):
    return step * 16 + layer


def flux_key(step, layer):
    return step * 16 + 8 + layer


def run_cut(space, steps, layers, src, stiff, buoy, pressure, velocity, put_load, put_flux):
    ends = (0, layers - 1)
    everywhere = tuple(range(layers))
    for k in range(steps):
        load = []
        for i in everywhere if k < steps - 1 else ends:
            p = src(k, i) if k == 0 else pressure[i] + src(k, i)
            pressure[i] = p
            load.append(stiff(i) * p)
        put_load(k, load[0])
        if k == steps - 1:
            put_flux(k, buoy(layers - 1) * (velocity[0, layers - 1] - load[-1]))
            return
        wanted = everywhere if k < steps - 2 else ends
        below = None
        for i in everywhere:
            x = (load[i + 1] - load[i]) if i + 1 < layers else -load[i]
            if k > 0:
                x = velocity[0, i] + x
            velocity[0, i] = x
            fx = buoy(i) * x
            if i == layers - 1:
                put_flux(k, fx)
            if i in wanted:
                y = space.fwd_y(load[i])
                z = space.fwd_z(load[i], load_key(k, i))
                if k > 0:
                    y, z = velocity[1, i] + y, velocity[2, i] + z
                velocity[1, i], velocity[2, i] = y, z
                spread = fx if i == 0 else fx - below
                spread = spread + space.bwd_y(buoy(i) * y)
                spread = spread + space.bwd_z(buoy(i) * z, flux_key(k, i))
                pressure[i] = pressure[i] + spread
            below = fx


def run_joined(space, steps, layers, src, stiff, buoy, pressure, velocity, load_in, flux_in, up, down, finished=None):
    everywhere = tuple(range(layers))
    above, under = layers, layers + 1
    pa = xa = ya = za = pa2 = None
    pb = xb = yb = zb = pb2 = xb2 = None
    for k in range(steps):
        inner = 0 < k < steps - 1
        load = []
        for i in everywhere:
            p = src(k, i) if k == 0 else pressure[i] + src(k, i)
            pressure[i] = p
            load.append(stiff(i) * p)
        beyond = load_in(k)
        if k > 0:
            la = up[0] * pa
            beyond = beyond + la
            lb = down[0] * pb
        if inner:
            xa = -la if xa is None else xa - la
            if pa2 is not None:
                xa = xa + up[1] * pa2
            y, z = space.fwd_y(la), space.fwd_z(la, load_key(k, above))
            ya, za = (y, z) if ya is None else (ya + y, za + z)
            y, z = space.fwd_y(lb), space.fwd_z(lb, load_key(k, under))
            yb, zb = (y, z) if yb is None else (yb + y, zb + z)
            xb2 = lb if xb2 is None else xb2 + lb
            if pb2 is not None:
                xb2 = xb2 - down[1] * pb2
        xb = load[0] if k == 0 else xb + load[0] - lb
        fb = down[2] * xb
        below = flux_in(k) + fb
        for i in everywhere:
            x = (load[i + 1] if i + 1 < layers else beyond) - load[i]
            y = space.fwd_y(load[i])
            z = space.fwd_z(load[i], load_key(k, i))
            if k > 0:
                x, y, z = velocity[0, i] + x, velocity[1, i] + y, velocity[2, i] + z
            velocity[0, i], velocity[1, i], velocity[2, i] = x, y, z
            fx = buoy(i) * x
            spread = fx - below
            spread = spread + space.bwd_y(buoy(i) * y)
            spread = spread + space.bwd_z(buoy(i) * z, flux_key(k, i))
            pressure[i] = pressure[i] + spread
            below = fx
            if k == steps - 1 and finished is not None:
                finished(i)
        if k == steps - 1:
            return
        if k == 0:
            pa, pb = -below, fb
            continue
        fa = up[2] * xa
        pa = pa + fa - below
        pa = pa + space.bwd_y(up[2] * ya) + space.bwd_z(up[2] * za, flux_key(k, above))
        fb2 = down[3] * xb2
        pb = pb + fb - fb2
        pb = pb + space.bwd_y(down[2] * yb) + space.bwd_z(down[2] * zb, flux_key(k, under))
        if k < steps - 2:
            pa2, pb2 = -fa, fb2


class Layers:
    def __init__(self, ref):
        self.ref = ref

    def __getitem__(self, i):
        return self.ref[i]

    def __setitem__(self, i, value):
        self.ref[i] = value


def pack_kernel(steps, layers, src, speed, imped, low, high, own):
    lanes = src.shape[-1]
    rows = layers * EDGE
    row, lane = iota((rows, lanes), 0), iota((rows, lanes), 1)
    wrow, wlane = iota((WIDE, lanes), 0), iota((WIDE, lanes), 1)
    half = WIDE // 2
    at_low = (wrow >= EDGE) & (wrow < half) & (wlane == wrow - EDGE)
    at_high = (wrow >= half) & (wrow < half + OWN) & (wlane == wrow + (lanes - OWN - half))
    wide = jnp.where(at_low | at_high, 1.0, 0.0)
    for f in range(steps + 2):
        total = None
        for i in range(layers):
            mine = (row >> 2) == i
            picks = [mine & (lane == base + (row & 3)) for base in (0, lanes - EDGE)]
            pick = jnp.concatenate([wide] + [jnp.where(p, 1.0, 0.0) for p in picks], 0).astype(jnp.bfloat16)
            if f < steps:
                block = brick_block(src, f, i).astype(jnp.bfloat16)
            else:
                block = (speed, imped)[f - steps][i]
            part = lax.dot_general(pick, block, (((1,), (1,)), ((), ())), preferred_element_type=jnp.float32)
            own[f, i * WIDE : (i + 1) * WIDE, :] = part[:WIDE]
            total = part[WIDE:] if total is None else total + part[WIDE:]
        low[f * rows : (f + 1) * rows, :] = total[:rows].astype(jnp.bfloat16)
        high[f * rows : (f + 1) * rows, :] = total[rows:].astype(jnp.bfloat16)


def strip_rows(message, at, lanes):
    parts = [f32(message[at + j * STRIP : at + (j + 1) * STRIP, :]) for j in range(lanes // 128)]
    return parts[0] if len(parts) == 1 else jnp.concatenate(parts, 1)


def put_strip(message, at, strip):
    for j in range(strip.shape[1] // 128):
        message[at + j * STRIP : at + (j + 1) * STRIP, :] = strip[:, j * 128 : (j + 1) * 128].astype(jnp.bfloat16)


def is_even():
    return lax.axis_index("gx") % 2 == 0


class Faces:
    def __init__(self, far, near):
        self.far, self.near = far, near
        self.even = is_even()

    def put(self, write, below, above):
        write(self.far, jnp.where(self.even, below, above))
        write(self.near, jnp.where(self.even, above, below))

    def above(self, read):
        return jnp.where(self.even, read(self.near), read(self.far))

    def below(self, read):
        return jnp.where(self.even, read(self.far), read(self.near))


def rows_writer(rows):
    def write(ref, k, a):
        ref[k * rows : (k + 1) * rows, :] = a.astype(jnp.bfloat16)
    return write


def rows_reader(rows):
    return lambda k: lambda ref: f32(ref[k * rows : (k + 1) * rows, :])


def strip_layout(steps, y):
    step = STRIP * (y // 128)
    return step, steps * y, steps * y + steps * step


def coefficients_kernel(speed, imped, stiff, buoy):
    for i in range(speed.shape[0]):
        stiff[i], buoy[i] = coefficients(f32(speed[i]), f32(imped[i]))


def cut_kernel(steps, layers, src, stiff, buoy, loads, fluxes, pressure, velocity):
    y, lanes = stiff.shape[1:]
    write = rows_writer(y)
    run_cut(
        Block((y, lanes), None), steps, layers, lambda k, i: brick_block(src, steps - 1 - k, i),
        lambda i: stiff[i], lambda i: buoy[i], Layers(pressure), Layers(velocity),
        lambda k, a: write(loads, k, a), lambda k, a: write(fluxes, k, a),
    )


def edge_kernel(
    steps, layers, gy_size, own, left, right, loads, fluxes, near, far, strips, whole, series, columns
):
    y, lanes = own.shape[2], loads.shape[1]
    rows = layers * EDGE
    me = lax.axis_index("gy")
    shape = (layers * WIDE, 2 * rows)
    r, c = iota(shape, 0), iota(shape, 1)
    inside = r & (WIDE - 1)
    at = (r >> 5) * EDGE + (r & 3)
    wanted = (inside < EDGE) & (c == at) & (me > 0)
    wanted = wanted | ((inside >= WIDE - EDGE) & (c == rows + at) & (me < gy_size - 1))
    order = jnp.where(wanted, 1.0, 0.0).astype(jnp.bfloat16)

    def narrow(a):
        half = STRIP // 2
        return jnp.concatenate([a[:half], a[WIDE - half :]], 0)

    for f in range(steps + 2):
        parts = jnp.concatenate([a[f * rows : (f + 1) * rows, :] for a in (left, right)], 0)
        whole[f] = own[f] + jnp.dot(order, parts, preferred_element_type=jnp.float32)
        for i in range(layers):
            strips[f, i * STRIP : (i + 1) * STRIP, :] = narrow(whole[f, i * WIDE : (i + 1) * WIDE, :])

    def strip(f, i):
        return whole[f, i * WIDE : (i + 1) * WIDE, :]

    faces = Faces(far, near)
    step, base, extra = strip_layout(steps, y)
    last = layers - 1
    for j, (f, depth) in enumerate(((steps, 0), (steps, 1), (steps + 1, 0), (steps + 1, 1))):
        faces.put(
            lambda ref, value, at=extra + j * step: put_strip(ref, at, value),
            narrow(strip(f, depth)), narrow(strip(f, last - depth)),
        )
    coef = [coefficients(strip(steps, i), strip(steps + 1, i)) for i in range(layers)]
    strip_loads, strip_fluxes = {}, {}
    run_cut(
        Strip((WIDE, y), None), steps, layers, lambda k, i: strip(steps - 1 - k, i),
        lambda i: coef[i][0], lambda i: coef[i][1], {}, {}, strip_loads.__setitem__, strip_fluxes.__setitem__,
    )
    outer = EDGE - 1
    series[...] = jnp.zeros(series.shape, jnp.float32)
    for k in range(steps):
        pair = narrow(strip_loads[k]), narrow(strip_fluxes[k])
        faces.put(lambda ref, value: put_strip(ref, base + k * step, value), *pair)
        if k > 0:
            for side, a in enumerate(pair):
                at = outer_key(k, side)
                series[at : at + outer, :] = a[HIGH - outer : HIGH, :]
                series[at + outer : at + 2 * outer, :] = a[LOW + 1 : LOW + 1 + outer, :]
    columns[...] = series[...].T

    lane = iota((y, lanes), 1)
    read, write = rows_reader(y), rows_writer(y)

    def merged(ref, k, side):
        a = read(k)(ref)
        if k == 0:
            return a
        placed = pltpu.roll(columns[...], (lanes - outer - outer_key(k, side)) % lanes, 1)
        return jnp.where((lane < k) | (lane >= lanes - k), placed, a)

    for k in range(steps):
        faces.put(lambda ref, value: write(ref, k, value), merged(loads, k, 0), merged(fluxes, k, 1))


def outer_key(step, side):
    return ((step - 1) * 2 + side) * 8


def joined_kernel(
    steps, layers, src, stiff, buoy, strips, near, far, coef_near, coef_far, pressure_out, velocity_out,
    pressure, velocity, series, columns, sems,
):
    y, lanes = stiff.shape[1:]

    def strip(f, i):
        return strips[f, i * STRIP : (i + 1) * STRIP, :]

    faces = Faces(far, near)
    step, base, extra = strip_layout(steps, y)

    def strip_at(at):
        return lambda ref: strip_rows(ref, at, y)

    def beside(side, at):
        s = [side(at(j)) for j in range(4)]
        (stiff, buoy), (stiff2, buoy2) = coefficients(s[0], s[2]), coefficients(s[1], s[3])
        return stiff, stiff2, buoy, buoy2

    coef = [coefficients(strip(steps, i), strip(steps + 1, i)) for i in range(layers)]
    series[...] = jnp.zeros(series.shape, jnp.float32)
    run_joined(
        Strip((STRIP, y), series), steps, layers, lambda k, i: strip(steps - 1 - k, i),
        lambda i: coef[i][0], lambda i: coef[i][1], {}, {},
        lambda k: faces.above(strip_at(base + k * step)), lambda k: faces.below(strip_at(base + k * step)),
        beside(faces.above, lambda j: strip_at(extra + j * step)),
        beside(faces.below, lambda j: strip_at(extra + j * step)),
    )
    columns[...] = series[...].T

    def copies(i):
        return (
            pltpu.make_async_copy(velocity.at[:, i], velocity_out.at[:, i], sems.at[0, i]),
            pltpu.make_async_copy(pressure.at[i], pressure_out.at[i], sems.at[1, i]),
        )

    def send(i):
        for copy in copies(i):
            copy.start()

    held = Faces(coef_far, coef_near)
    read = rows_reader(y)
    run_joined(
        Block((y, lanes), columns), steps, layers, lambda k, i: brick_block(src, steps - 1 - k, i),
        lambda i: stiff[i], lambda i: buoy[i], Layers(pressure), Layers(velocity),
        lambda k: faces.above(read(k)), lambda k: faces.below(read(k)),
        beside(held.above, lambda j: lambda ref: f32(ref[j])),
        beside(held.below, lambda j: lambda ref: f32(ref[j])),
        send,
    )
    for i in range(layers):
        for copy in copies(i):
            copy.wait()


def shifted(block, axis, distance):
    devices = range(lax.axis_size(axis))
    return lax.ppermute(block, axis, [(i, i + distance) for i in devices if i + distance in devices])


def swapped(block, axis, first):
    pairs = [(i, i + 1) for i in range(first, lax.axis_size(axis) - 1, 2)]
    return lax.ppermute(block, axis, pairs + [(j, i) for i, j in pairs])


def on_device(source, speed, impedance):
    steps, whole_x, brick_y, lanes = source.shape
    layers, y, _ = speed.shape
    assert layers == steps == EDGE and lanes == 128 and y % 128 == 0
    gy_size = lax.axis_size("gy")
    xs = ("grp", "gx")
    bf16 = jnp.bfloat16
    params = pltpu.CompilerParams(vmem_limit_bytes=32 * 1024 * 1024)
    sds = jax.ShapeDtypeStruct

    assert lax.axis_size("gx") % 2 == 0
    below = jnp.concatenate([speed[:2], impedance[:2]], 0)
    above = jnp.concatenate([speed[-1:], speed[-2:-1], impedance[-1:], impedance[-2:-1]], 0)
    even = is_even()
    coef_far, coef_near = jnp.where(even, below, above), jnp.where(even, above, below)
    coef_far, coef_near = swapped(coef_far, xs, 1), swapped(coef_near, xs, 0)
    relaid = lax.all_to_all(source.transpose(1, 0, 2, 3), xs, split_axis=0, concat_axis=0, tiled=True)
    relaid = relaid.reshape(whole_x // layers, layers, steps, brick_y, lanes)
    field = sds((layers, y, lanes), jnp.float32)
    stiff, buoy = pl.pallas_call(
        coefficients_kernel, out_shape=(field, field), compiler_params=params, name="coefficients"
    )(speed, impedance)
    relaid, coef_far, coef_near, stiff, buoy = lax.optimization_barrier((relaid, coef_far, coef_near, stiff, buoy))

    def call(kernel, outs, scratch, *args, name):
        return pl.pallas_call(kernel, out_shape=outs, scratch_shapes=scratch, compiler_params=params, name=name)(*args)

    edge = sds(((steps + 2) * layers * EDGE, y), bf16)
    low, high, own = call(
        functools.partial(pack_kernel, steps, layers),
        (edge, edge, sds((steps + 2, layers * WIDE, y), jnp.float32)), [], relaid, speed, impedance, name="pack",
    )
    if gy_size == 2:
        left = right = lax.ppermute(jnp.where(lax.axis_index("gy") == 0, high, low), "gy", [(0, 1), (1, 0)])
    else:
        left, right = shifted(high, "gy", 1), shifted(low, "gy", -1)

    whole = pltpu.VMEM((layers, y, lanes), jnp.float32)
    whole_velocity = pltpu.VMEM((3, layers, y, lanes), jnp.float32)
    series = [pltpu.VMEM((128, y), jnp.float32), pltpu.VMEM((y, 128), jnp.float32)]
    face = sds((steps * y, 128), bf16)
    loads, fluxes = call(
        functools.partial(cut_kernel, steps, layers), (face, face), [whole, whole_velocity], relaid, stiff, buoy, name="cut"
    )
    _, _, extra = strip_layout(steps, y)
    message = sds((extra + 4 * STRIP * (y // 128), 128), bf16)
    near, far, strips = call(
        functools.partial(edge_kernel, steps, layers, gy_size),
        (message, message, sds((steps + 2, layers * STRIP, y), jnp.float32)),
        [pltpu.VMEM((steps + 2, layers * WIDE, y), jnp.float32)] + series,
        own, left, right, loads, fluxes, name="edge",
    )
    near = swapped(near, xs, 0)
    far = swapped(far, xs, 1)

    args = relaid, stiff, buoy, strips, near, far, coef_near, coef_far
    return pl.pallas_call(
        functools.partial(joined_kernel, steps, layers),
        in_specs=[pl.BlockSpec(memory_space=pltpu.VMEM)] * len(args),
        out_specs=(pl.BlockSpec(memory_space=pl.ANY), pl.BlockSpec(memory_space=pl.ANY)),
        out_shape=(field, sds((3, layers, y, lanes), jnp.float32)),
        scratch_shapes=[whole, whole_velocity] + series + [pltpu.SemaphoreType.DMA((2, layers))],
        compiler_params=params,
        name="joined",
    )(*args)


def solution(mesh):
    in_specs = (
        P(None, None, ("grp", "gx"), "gy"),
        P(("grp", "gx"), None, "gy"),
        P(("grp", "gx"), None, "gy"),
    )
    out_specs = (P(("grp", "gx"), None, "gy"), P(None, ("grp", "gx"), None, "gy"))
    return jax.shard_map(
        on_device, mesh=mesh, in_specs=in_specs, out_specs=out_specs, check_vma=False
    )
```

```python
import functools

import jax
import jax.numpy as jnp
from jax import lax
from jax.experimental import pallas as pl
from jax.experimental.pallas import tpu as pltpu
from jax.sharding import PartitionSpec as P

courant = 0.15
EDGE = 4
STRIP = 4 * EDGE
OWN = 3 * EDGE
WIDE = 2 * (OWN + EDGE)
LOW, HIGH = EDGE - 1, 3 * EDGE


def f32(x):
    return x.astype(jnp.float32)


def iota(shape, dim):
    return lax.broadcasted_iota(jnp.int32, shape, dim)


def brick_block(src, step, layer):
    bricks = f32(src[:, layer, step])
    return bricks.reshape(bricks.shape[0] * bricks.shape[1], bricks.shape[2])


def coefficients(speed, imped):
    held = imped > 0.0
    stiff = courant * (speed * imped)
    buoy = jnp.where(held, courant * (speed / jnp.where(held, imped, 1.0)), 0.0)
    return stiff, buoy


class Block:
    def __init__(self, shape, series):
        self.row, self.lane = iota(shape, 0), iota(shape, 1)
        self.rows, self.lanes = shape
        self.series = series

    def fwd_y(self, a):
        return jnp.where(self.row == self.rows - 1, 0.0, pltpu.roll(a, self.rows - 1, 0)) - a

    def bwd_y(self, g):
        return g - jnp.where(self.row == 0, 0.0, pltpu.roll(g, 1, 0))

    def column(self, key):
        return 0.0 if self.series is None else self.series[:, key : key + 1]

    def fwd_z(self, a, key):
        col = self.column(key)
        return jnp.where(self.lane == self.lanes - 1, col, pltpu.roll(a, self.lanes - 1, 1)) - a

    def bwd_z(self, g, key):
        col = self.column(key)
        return g - jnp.where(self.lane == 0, col, pltpu.roll(g, 1, 1))


class Strip:
    def __init__(self, shape, series):
        self.lane = iota(shape, 1)
        self.rows, self.lanes = shape
        self.series = series

    def fwd_y(self, a):
        return jnp.where(self.lane == self.lanes - 1, 0.0, pltpu.roll(a, self.lanes - 1, 1)) - a

    def bwd_y(self, g):
        return g - jnp.where(self.lane == 0, 0.0, pltpu.roll(g, 1, 1))

    def fwd_z(self, a, key):
        if self.series is not None:
            self.series[key : key + 1, :] = a[HIGH : HIGH + 1, :]
        return pltpu.roll(a, self.rows - 1, 0) - a

    def bwd_z(self, g, key):
        if self.series is not None:
            self.series[key : key + 1, :] = g[LOW : LOW + 1, :]
        return g - pltpu.roll(g, 1, 0)


def load_key(step, layer):
    return step * 16 + layer


def flux_key(step, layer):
    return step * 16 + 8 + layer


def run_cut(space, steps, layers, src, stiff, buoy, pressure, velocity, put_load, put_flux):
    ends = (0, layers - 1)
    everywhere = tuple(range(layers))
    for k in range(steps):
        load = []
        for i in everywhere if k < steps - 1 else ends:
            p = src(k, i) if k == 0 else pressure[i] + src(k, i)
            pressure[i] = p
            load.append(stiff(i) * p)
        put_load(k, load[0])
        if k == steps - 1:
            put_flux(k, buoy(layers - 1) * (velocity[0, layers - 1] - load[-1]))
            return
        wanted = everywhere if k < steps - 2 else ends
        below = None
        for i in everywhere:
            x = (load[i + 1] - load[i]) if i + 1 < layers else -load[i]
            if k > 0:
                x = velocity[0, i] + x
            velocity[0, i] = x
            fx = buoy(i) * x
            if i == layers - 1:
                put_flux(k, fx)
            if i in wanted:
                y = space.fwd_y(load[i])
                z = space.fwd_z(load[i], load_key(k, i))
                if k > 0:
                    y, z = velocity[1, i] + y, velocity[2, i] + z
                velocity[1, i], velocity[2, i] = y, z
                spread = fx if i == 0 else fx - below
                spread = spread + space.bwd_y(buoy(i) * y)
                spread = spread + space.bwd_z(buoy(i) * z, flux_key(k, i))
                pressure[i] = pressure[i] + spread
            below = fx


def run_joined(space, steps, layers, src, stiff, buoy, pressure, velocity, load_in, flux_in, up, down, finished=None):
    everywhere = tuple(range(layers))
    above, under = layers, layers + 1
    pa = xa = ya = za = pa2 = None
    pb = xb = yb = zb = pb2 = xb2 = None
    for k in range(steps):
        inner = 0 < k < steps - 1
        load = []
        for i in everywhere:
            p = src(k, i) if k == 0 else pressure[i] + src(k, i)
            pressure[i] = p
            load.append(stiff(i) * p)
        beyond = load_in(k)
        if k > 0:
            la = up[0] * pa
            beyond = beyond + la
            lb = down[0] * pb
        if inner:
            xa = -la if xa is None else xa - la
            if pa2 is not None:
                xa = xa + up[1] * pa2
            y, z = space.fwd_y(la), space.fwd_z(la, load_key(k, above))
            ya, za = (y, z) if ya is None else (ya + y, za + z)
            y, z = space.fwd_y(lb), space.fwd_z(lb, load_key(k, under))
            yb, zb = (y, z) if yb is None else (yb + y, zb + z)
            xb2 = lb if xb2 is None else xb2 + lb
            if pb2 is not None:
                xb2 = xb2 - down[1] * pb2
        xb = load[0] if k == 0 else xb + load[0] - lb
        fb = down[2] * xb
        below = flux_in(k) + fb
        for i in everywhere:
            x = (load[i + 1] if i + 1 < layers else beyond) - load[i]
            y = space.fwd_y(load[i])
            z = space.fwd_z(load[i], load_key(k, i))
            if k > 0:
                x, y, z = velocity[0, i] + x, velocity[1, i] + y, velocity[2, i] + z
            velocity[0, i], velocity[1, i], velocity[2, i] = x, y, z
            fx = buoy(i) * x
            spread = fx - below
            spread = spread + space.bwd_y(buoy(i) * y)
            spread = spread + space.bwd_z(buoy(i) * z, flux_key(k, i))
            pressure[i] = pressure[i] + spread
            below = fx
            if k == steps - 1 and finished is not None:
                finished(i)
        if k == steps - 1:
            return
        if k == 0:
            pa, pb = -below, fb
            continue
        fa = up[2] * xa
        pa = pa + fa - below
        pa = pa + space.bwd_y(up[2] * ya) + space.bwd_z(up[2] * za, flux_key(k, above))
        fb2 = down[3] * xb2
        pb = pb + fb - fb2
        pb = pb + space.bwd_y(down[2] * yb) + space.bwd_z(down[2] * zb, flux_key(k, under))
        if k < steps - 2:
            pa2, pb2 = -fa, fb2


class Layers:
    def __init__(self, ref):
        self.ref = ref

    def __getitem__(self, i):
        return self.ref[i]

    def __setitem__(self, i, value):
        self.ref[i] = value


def pack_kernel(steps, layers, src, speed, imped, coef_near, coef_far, low, high, own):
    lanes = src.shape[-1]
    rows = layers * EDGE
    row, lane = iota((rows, lanes), 0), iota((rows, lanes), 1)
    wrow, wlane = iota((WIDE, lanes), 0), iota((WIDE, lanes), 1)
    half = WIDE // 2
    at_low = (wrow >= EDGE) & (wrow < half) & (wlane == wrow - EDGE)
    at_high = (wrow >= half) & (wrow < half + OWN) & (wlane == wrow + (lanes - OWN - half))
    wide = jnp.where(at_low | at_high, 1.0, 0.0)
    for f in range(steps + 4):
        total = None
        for i in range(layers):
            mine = (row >> 2) == i
            picks = [mine & (lane == base + (row & 3)) for base in (0, lanes - EDGE)]
            pick = jnp.concatenate([wide] + [jnp.where(p, 1.0, 0.0) for p in picks], 0).astype(jnp.bfloat16)
            if f < steps:
                block = brick_block(src, f, i).astype(jnp.bfloat16)
            else:
                block = (speed, imped, coef_near, coef_far)[f - steps][i]
            part = lax.dot_general(pick, block, (((1,), (1,)), ((), ())), preferred_element_type=jnp.float32)
            own[f, i * WIDE : (i + 1) * WIDE, :] = part[:WIDE]
            total = part[WIDE:] if total is None else total + part[WIDE:]
        low[f * rows : (f + 1) * rows, :] = total[:rows].astype(jnp.bfloat16)
        high[f * rows : (f + 1) * rows, :] = total[rows:].astype(jnp.bfloat16)


def strip_rows(message, at, lanes):
    parts = [f32(message[at + j * STRIP : at + (j + 1) * STRIP, :]) for j in range(lanes // 128)]
    return parts[0] if len(parts) == 1 else jnp.concatenate(parts, 1)


def put_strip(message, at, strip):
    for j in range(strip.shape[1] // 128):
        message[at + j * STRIP : at + (j + 1) * STRIP, :] = strip[:, j * 128 : (j + 1) * 128].astype(jnp.bfloat16)


def is_even():
    return lax.axis_index("gx") % 2 == 0


class Faces:
    def __init__(self, far, near):
        self.far, self.near = far, near
        self.even = is_even()

    def put(self, write, below, above):
        write(self.far, jnp.where(self.even, below, above))
        write(self.near, jnp.where(self.even, above, below))

    def above(self, read):
        return jnp.where(self.even, read(self.near), read(self.far))

    def below(self, read):
        return jnp.where(self.even, read(self.far), read(self.near))


def rows_writer(rows):
    def write(ref, k, a):
        ref[k * rows : (k + 1) * rows, :] = a.astype(jnp.bfloat16)
    return write


def rows_reader(rows):
    return lambda k: lambda ref: f32(ref[k * rows : (k + 1) * rows, :])


def strip_layout(steps, y):
    step = STRIP * (y // 128)
    return step, steps * y, steps * y + steps * step


def coefficients_kernel(speed, imped, stiff, buoy, near, far):
    faces = Faces(far, near)
    last = speed.shape[0] - 1
    for j, ref in enumerate((speed, imped)):
        for depth in range(2):
            def write(out, value, at=2 * j + depth):
                out[at] = value.astype(jnp.bfloat16)
            faces.put(write, f32(ref[depth]), f32(ref[last - depth]))
    for i in range(last + 1):
        stiff[i], buoy[i] = coefficients(f32(speed[i]), f32(imped[i]))


def cut_kernel(steps, layers, src, stiff, buoy, loads, fluxes, pressure, velocity):
    y, lanes = stiff.shape[1:]
    write = rows_writer(y)
    run_cut(
        Block((y, lanes), None), steps, layers, lambda k, i: brick_block(src, steps - 1 - k, i),
        lambda i: stiff[i], lambda i: buoy[i], Layers(pressure), Layers(velocity),
        lambda k, a: write(loads, k, a), lambda k, a: write(fluxes, k, a),
    )


def edge_kernel(
    steps, layers, gy_size, own, left, right, loads, fluxes, near, far, strips, whole, series, columns
):
    y, lanes = own.shape[2], loads.shape[1]
    rows = layers * EDGE
    me = lax.axis_index("gy")
    shape = (layers * WIDE, 2 * rows)
    r, c = iota(shape, 0), iota(shape, 1)
    inside = r & (WIDE - 1)
    at = (r >> 5) * EDGE + (r & 3)
    wanted = (inside < EDGE) & (c == at) & (me > 0)
    wanted = wanted | ((inside >= WIDE - EDGE) & (c == rows + at) & (me < gy_size - 1))
    order = jnp.where(wanted, 1.0, 0.0).astype(jnp.bfloat16)

    def narrow(a):
        half = STRIP // 2
        return jnp.concatenate([a[:half], a[WIDE - half :]], 0)

    for f in range(steps + 4):
        parts = jnp.concatenate([a[f * rows : (f + 1) * rows, :] for a in (left, right)], 0)
        whole[f] = own[f] + jnp.dot(order, parts, preferred_element_type=jnp.float32)
        for i in range(layers):
            strips[f, i * STRIP : (i + 1) * STRIP, :] = narrow(whole[f, i * WIDE : (i + 1) * WIDE, :])

    def strip(f, i):
        return whole[f, i * WIDE : (i + 1) * WIDE, :]

    faces = Faces(far, near)
    step, base, _ = strip_layout(steps, y)
    coef = [coefficients(strip(steps, i), strip(steps + 1, i)) for i in range(layers)]
    strip_loads, strip_fluxes = {}, {}
    run_cut(
        Strip((WIDE, y), None), steps, layers, lambda k, i: strip(steps - 1 - k, i),
        lambda i: coef[i][0], lambda i: coef[i][1], {}, {}, strip_loads.__setitem__, strip_fluxes.__setitem__,
    )
    outer = EDGE - 1
    series[...] = jnp.zeros(series.shape, jnp.float32)
    for k in range(steps):
        pair = narrow(strip_loads[k]), narrow(strip_fluxes[k])
        faces.put(lambda ref, value: put_strip(ref, base + k * step, value), *pair)
        if k > 0:
            for side, a in enumerate(pair):
                at = outer_key(k, side)
                series[at : at + outer, :] = a[HIGH - outer : HIGH, :]
                series[at + outer : at + 2 * outer, :] = a[LOW + 1 : LOW + 1 + outer, :]
    columns[...] = series[...].T

    lane = iota((y, lanes), 1)
    read, write = rows_reader(y), rows_writer(y)

    def merged(ref, k, side):
        a = read(k)(ref)
        if k == 0:
            return a
        placed = pltpu.roll(columns[...], (lanes - outer - outer_key(k, side)) % lanes, 1)
        return jnp.where((lane < k) | (lane >= lanes - k), placed, a)

    for k in range(steps):
        faces.put(lambda ref, value: write(ref, k, value), merged(loads, k, 0), merged(fluxes, k, 1))


def outer_key(step, side):
    return ((step - 1) * 2 + side) * 8


def joined_kernel(
    steps, layers, src, stiff, buoy, strips, near, far, coef_near, coef_far, pressure_out, velocity_out,
    pressure, velocity, series, columns, sems,
):
    y, lanes = stiff.shape[1:]

    def strip(f, i):
        return strips[f, i * STRIP : (i + 1) * STRIP, :]

    faces = Faces(far, near)
    step, base, _ = strip_layout(steps, y)
    held = Faces(coef_far, coef_near)
    edge_held = Faces(steps + 3, steps + 2)

    def strip_at(at):
        return lambda ref: strip_rows(ref, at, y)

    def beside(side, at):
        s = [side(at(j)) for j in range(4)]
        (stiff, buoy), (stiff2, buoy2) = coefficients(s[0], s[2]), coefficients(s[1], s[3])
        return stiff, stiff2, buoy, buoy2

    coef = [coefficients(strip(steps, i), strip(steps + 1, i)) for i in range(layers)]
    series[...] = jnp.zeros(series.shape, jnp.float32)
    run_joined(
        Strip((STRIP, y), series), steps, layers, lambda k, i: strip(steps - 1 - k, i),
        lambda i: coef[i][0], lambda i: coef[i][1], {}, {},
        lambda k: faces.above(strip_at(base + k * step)), lambda k: faces.below(strip_at(base + k * step)),
        beside(edge_held.above, lambda j: lambda f: strip(f, j)),
        beside(edge_held.below, lambda j: lambda f: strip(f, j)),
    )
    columns[...] = series[...].T

    def copies(i):
        return (
            pltpu.make_async_copy(velocity.at[:, i], velocity_out.at[:, i], sems.at[0, i]),
            pltpu.make_async_copy(pressure.at[i], pressure_out.at[i], sems.at[1, i]),
        )

    def send(i):
        for copy in copies(i):
            copy.start()

    read = rows_reader(y)
    run_joined(
        Block((y, lanes), columns), steps, layers, lambda k, i: brick_block(src, steps - 1 - k, i),
        lambda i: stiff[i], lambda i: buoy[i], Layers(pressure), Layers(velocity),
        lambda k: faces.above(read(k)), lambda k: faces.below(read(k)),
        beside(held.above, lambda j: lambda ref: f32(ref[j])),
        beside(held.below, lambda j: lambda ref: f32(ref[j])),
        send,
    )
    for i in range(layers):
        for copy in copies(i):
            copy.wait()


def shifted(block, axis, distance):
    devices = range(lax.axis_size(axis))
    return lax.ppermute(block, axis, [(i, i + distance) for i in devices if i + distance in devices])


def swapped(block, axis, first):
    pairs = [(i, i + 1) for i in range(first, lax.axis_size(axis) - 1, 2)]
    return lax.ppermute(block, axis, pairs + [(j, i) for i, j in pairs])


def on_device(source, speed, impedance):
    steps, whole_x, brick_y, lanes = source.shape
    layers, y, _ = speed.shape
    assert layers == steps == EDGE and lanes == 128 and y % 128 == 0
    gy_size = lax.axis_size("gy")
    xs = ("grp", "gx")
    bf16 = jnp.bfloat16
    params = pltpu.CompilerParams(vmem_limit_bytes=32 * 1024 * 1024)
    sds = jax.ShapeDtypeStruct

    assert lax.axis_size("gx") % 2 == 0
    field, coef = sds((layers, y, lanes), jnp.float32), sds((4, y, lanes), bf16)
    stiff, buoy, coef_near, coef_far = pl.pallas_call(
        coefficients_kernel, out_shape=(field, field, coef, coef), compiler_params=params, name="coefficients"
    )(speed, impedance)
    coef_near, coef_far = swapped(coef_near, xs, 0), swapped(coef_far, xs, 1)
    relaid = lax.all_to_all(source.transpose(1, 0, 2, 3), xs, split_axis=0, concat_axis=0, tiled=True)
    relaid = relaid.reshape(whole_x // layers, layers, steps, brick_y, lanes)
    relaid, coef_near, coef_far, stiff, buoy = lax.optimization_barrier((relaid, coef_near, coef_far, stiff, buoy))

    def call(kernel, outs, scratch, *args, name):
        return pl.pallas_call(kernel, out_shape=outs, scratch_shapes=scratch, compiler_params=params, name=name)(*args)

    edge = sds(((steps + 4) * layers * EDGE, y), bf16)
    low, high, own = call(
        functools.partial(pack_kernel, steps, layers),
        (edge, edge, sds((steps + 4, layers * WIDE, y), jnp.float32)), [],
        relaid, speed, impedance, coef_near, coef_far, name="pack",
    )
    if gy_size == 2:
        left = right = lax.ppermute(jnp.where(lax.axis_index("gy") == 0, high, low), "gy", [(0, 1), (1, 0)])
    else:
        left, right = shifted(high, "gy", 1), shifted(low, "gy", -1)

    whole = pltpu.VMEM((layers, y, lanes), jnp.float32)
    whole_velocity = pltpu.VMEM((3, layers, y, lanes), jnp.float32)
    series = [pltpu.VMEM((128, y), jnp.float32), pltpu.VMEM((y, 128), jnp.float32)]
    face = sds((steps * y, 128), bf16)
    loads, fluxes = call(
        functools.partial(cut_kernel, steps, layers), (face, face), [whole, whole_velocity], relaid, stiff, buoy, name="cut"
    )
    message = sds((strip_layout(steps, y)[2], 128), bf16)
    near, far, strips = call(
        functools.partial(edge_kernel, steps, layers, gy_size),
        (message, message, sds((steps + 4, layers * STRIP, y), jnp.float32)),
        [pltpu.VMEM((steps + 4, layers * WIDE, y), jnp.float32)] + series,
        own, left, right, loads, fluxes, name="edge",
    )
    near = swapped(near, xs, 0)
    far = swapped(far, xs, 1)

    args = relaid, stiff, buoy, strips, near, far, coef_near, coef_far
    return pl.pallas_call(
        functools.partial(joined_kernel, steps, layers),
        in_specs=[pl.BlockSpec(memory_space=pltpu.VMEM)] * len(args),
        out_specs=(pl.BlockSpec(memory_space=pl.ANY), pl.BlockSpec(memory_space=pl.ANY)),
        out_shape=(field, sds((3, layers, y, lanes), jnp.float32)),
        scratch_shapes=[whole, whole_velocity] + series + [pltpu.SemaphoreType.DMA((2, layers))],
        compiler_params=params,
        name="joined",
    )(*args)


def solution(mesh):
    in_specs = (
        P(None, None, ("grp", "gx"), "gy"),
        P(("grp", "gx"), None, "gy"),
        P(("grp", "gx"), None, "gy"),
    )
    out_specs = (P(("grp", "gx"), None, "gy"), P(None, ("grp", "gx"), None, "gy"))
    return jax.shard_map(
        on_device, mesh=mesh, in_specs=in_specs, out_specs=out_specs, check_vma=False
    )
```

```python
import functools

import jax
import jax.numpy as jnp
from jax import lax
from jax.experimental import pallas as pl
from jax.experimental.pallas import tpu as pltpu
from jax.sharding import PartitionSpec as P

courant = 0.15
EDGE = 4
STRIP = 4 * EDGE
OWN = 3 * EDGE
WIDE = 2 * (OWN + EDGE)
LOW, HIGH = EDGE - 1, 3 * EDGE


def f32(x):
    return x.astype(jnp.float32)


def iota(shape, dim):
    return lax.broadcasted_iota(jnp.int32, shape, dim)


def brick_block(src, step, layer):
    bricks = f32(src[:, layer, step])
    return bricks.reshape(bricks.shape[0] * bricks.shape[1], bricks.shape[2])


def coefficients(speed, imped):
    held = imped > 0.0
    stiff = courant * (speed * imped)
    buoy = jnp.where(held, courant * (speed / jnp.where(held, imped, 1.0)), 0.0)
    return stiff, buoy


class Block:
    def __init__(self, shape, series):
        self.row, self.lane = iota(shape, 0), iota(shape, 1)
        self.rows, self.lanes = shape
        self.series = series

    def fwd_y(self, a):
        return jnp.where(self.row == self.rows - 1, 0.0, pltpu.roll(a, self.rows - 1, 0)) - a

    def bwd_y(self, g):
        return g - jnp.where(self.row == 0, 0.0, pltpu.roll(g, 1, 0))

    def column(self, key):
        return 0.0 if self.series is None else self.series[:, key : key + 1]

    def fwd_z(self, a, key):
        col = self.column(key)
        return jnp.where(self.lane == self.lanes - 1, col, pltpu.roll(a, self.lanes - 1, 1)) - a

    def bwd_z(self, g, key):
        col = self.column(key)
        return g - jnp.where(self.lane == 0, col, pltpu.roll(g, 1, 1))


class Strip:
    def __init__(self, shape, series):
        self.lane = iota(shape, 1)
        self.rows, self.lanes = shape
        self.series = series

    def fwd_y(self, a):
        return jnp.where(self.lane == self.lanes - 1, 0.0, pltpu.roll(a, self.lanes - 1, 1)) - a

    def bwd_y(self, g):
        return g - jnp.where(self.lane == 0, 0.0, pltpu.roll(g, 1, 1))

    def fwd_z(self, a, key):
        if self.series is not None:
            self.series[key : key + 1, :] = a[HIGH : HIGH + 1, :]
        return pltpu.roll(a, self.rows - 1, 0) - a

    def bwd_z(self, g, key):
        if self.series is not None:
            self.series[key : key + 1, :] = g[LOW : LOW + 1, :]
        return g - pltpu.roll(g, 1, 0)


def load_key(step, layer):
    return step * 16 + layer


def flux_key(step, layer):
    return step * 16 + 8 + layer


def run_cut(space, steps, layers, src, stiff, buoy, pressure, velocity, put_load, put_flux):
    ends = (0, layers - 1)
    everywhere = tuple(range(layers))
    for k in range(steps):
        load = []
        for i in everywhere if k < steps - 1 else ends:
            p = src(k, i) if k == 0 else pressure[i] + src(k, i)
            pressure[i] = p
            load.append(stiff(i) * p)
        put_load(k, load[0])
        if k == steps - 1:
            put_flux(k, buoy(layers - 1) * (velocity[0, layers - 1] - load[-1]))
            return
        wanted = everywhere if k < steps - 2 else ends
        below = None
        for i in everywhere:
            x = (load[i + 1] - load[i]) if i + 1 < layers else -load[i]
            if k > 0:
                x = velocity[0, i] + x
            velocity[0, i] = x
            fx = buoy(i) * x
            if i == layers - 1:
                put_flux(k, fx)
            if i in wanted:
                y = space.fwd_y(load[i])
                z = space.fwd_z(load[i], load_key(k, i))
                if k > 0:
                    y, z = velocity[1, i] + y, velocity[2, i] + z
                velocity[1, i], velocity[2, i] = y, z
                spread = fx if i == 0 else fx - below
                spread = spread + space.bwd_y(buoy(i) * y)
                spread = spread + space.bwd_z(buoy(i) * z, flux_key(k, i))
                pressure[i] = pressure[i] + spread
            below = fx


def run_joined(space, steps, layers, src, stiff, buoy, pressure, velocity, load_in, flux_in, up, down, finished=None):
    everywhere = tuple(range(layers))
    above, under = layers, layers + 1
    pa = xa = ya = za = pa2 = None
    pb = xb = yb = zb = pb2 = xb2 = None
    for k in range(steps):
        inner = 0 < k < steps - 1
        load = []
        for i in everywhere:
            p = src(k, i) if k == 0 else pressure[i] + src(k, i)
            pressure[i] = p
            load.append(stiff(i) * p)
        beyond = load_in(k)
        if k > 0:
            la = up[0] * pa
            beyond = beyond + la
            lb = down[0] * pb
        if inner:
            xa = -la if xa is None else xa - la
            if pa2 is not None:
                xa = xa + up[1] * pa2
            y, z = space.fwd_y(la), space.fwd_z(la, load_key(k, above))
            ya, za = (y, z) if ya is None else (ya + y, za + z)
            y, z = space.fwd_y(lb), space.fwd_z(lb, load_key(k, under))
            yb, zb = (y, z) if yb is None else (yb + y, zb + z)
            xb2 = lb if xb2 is None else xb2 + lb
            if pb2 is not None:
                xb2 = xb2 - down[1] * pb2
        xb = load[0] if k == 0 else xb + load[0] - lb
        fb = down[2] * xb
        below = flux_in(k) + fb
        for i in everywhere:
            x = (load[i + 1] if i + 1 < layers else beyond) - load[i]
            y = space.fwd_y(load[i])
            z = space.fwd_z(load[i], load_key(k, i))
            if k > 0:
                x, y, z = velocity[0, i] + x, velocity[1, i] + y, velocity[2, i] + z
            velocity[0, i], velocity[1, i], velocity[2, i] = x, y, z
            fx = buoy(i) * x
            spread = fx - below
            spread = spread + space.bwd_y(buoy(i) * y)
            spread = spread + space.bwd_z(buoy(i) * z, flux_key(k, i))
            pressure[i] = pressure[i] + spread
            below = fx
            if k == steps - 1 and finished is not None:
                finished(i)
        if k == steps - 1:
            return
        if k == 0:
            pa, pb = -below, fb
            continue
        fa = up[2] * xa
        pa = pa + fa - below
        pa = pa + space.bwd_y(up[2] * ya) + space.bwd_z(up[2] * za, flux_key(k, above))
        fb2 = down[3] * xb2
        pb = pb + fb - fb2
        pb = pb + space.bwd_y(down[2] * yb) + space.bwd_z(down[2] * zb, flux_key(k, under))
        if k < steps - 2:
            pa2, pb2 = -fa, fb2


class Layers:
    def __init__(self, ref):
        self.ref = ref

    def __getitem__(self, i):
        return self.ref[i]

    def __setitem__(self, i, value):
        self.ref[i] = value


def field_block(steps, src, fields, f, i):
    return brick_block(src, f, i).astype(jnp.bfloat16) if f < steps else fields[f - steps][i]


def picked(pick, block):
    return lax.dot_general(pick, block, (((1,), (1,)), ((), ())), preferred_element_type=jnp.float32)


def pack_kernel(steps, layers, src, speed, imped, coef_near, coef_far, low, high):
    lanes = src.shape[-1]
    rows = layers * EDGE
    row, lane = iota((rows, lanes), 0), iota((rows, lanes), 1)
    fields = speed, imped, coef_near, coef_far
    for f in range(steps + 4):
        total = None
        for i in range(layers):
            mine = (row >> 2) == i
            picks = [mine & (lane == base + (row & 3)) for base in (0, lanes - EDGE)]
            pick = jnp.concatenate([jnp.where(p, 1.0, 0.0) for p in picks], 0).astype(jnp.bfloat16)
            part = picked(pick, field_block(steps, src, fields, f, i))
            total = part if total is None else total + part
        low[f * rows : (f + 1) * rows, :] = total[:rows].astype(jnp.bfloat16)
        high[f * rows : (f + 1) * rows, :] = total[rows:].astype(jnp.bfloat16)


def own_kernel(steps, layers, src, speed, imped, coef_near, coef_far, own):
    lanes = src.shape[-1]
    wrow, wlane = iota((WIDE, lanes), 0), iota((WIDE, lanes), 1)
    half = WIDE // 2
    at_low = (wrow >= EDGE) & (wrow < half) & (wlane == wrow - EDGE)
    at_high = (wrow >= half) & (wrow < half + OWN) & (wlane == wrow + (lanes - OWN - half))
    wide = jnp.where(at_low | at_high, 1.0, 0.0).astype(jnp.bfloat16)
    fields = speed, imped, coef_near, coef_far
    for f in range(steps + 4):
        for i in range(layers):
            own[f, i * WIDE : (i + 1) * WIDE, :] = picked(wide, field_block(steps, src, fields, f, i))


def strip_rows(message, at, lanes):
    parts = [f32(message[at + j * STRIP : at + (j + 1) * STRIP, :]) for j in range(lanes // 128)]
    return parts[0] if len(parts) == 1 else jnp.concatenate(parts, 1)


def put_strip(message, at, strip):
    for j in range(strip.shape[1] // 128):
        message[at + j * STRIP : at + (j + 1) * STRIP, :] = strip[:, j * 128 : (j + 1) * 128].astype(jnp.bfloat16)


def is_even():
    return lax.axis_index("gx") % 2 == 0


class Faces:
    def __init__(self, far, near):
        self.far, self.near = far, near
        self.even = is_even()

    def put(self, write, below, above):
        write(self.far, jnp.where(self.even, below, above))
        write(self.near, jnp.where(self.even, above, below))

    def above(self, read):
        return jnp.where(self.even, read(self.near), read(self.far))

    def below(self, read):
        return jnp.where(self.even, read(self.far), read(self.near))


def rows_writer(rows):
    def write(ref, k, a):
        ref[k * rows : (k + 1) * rows, :] = a.astype(jnp.bfloat16)
    return write


def rows_reader(rows):
    return lambda k: lambda ref: f32(ref[k * rows : (k + 1) * rows, :])


def strip_layout(steps, y):
    step = STRIP * (y // 128)
    return step, steps * y, steps * y + steps * step


def coefficients_kernel(speed, imped, stiff, buoy, near, far):
    faces = Faces(far, near)
    last = speed.shape[0] - 1
    for j, ref in enumerate((speed, imped)):
        for depth in range(2):
            def write(out, value, at=2 * j + depth):
                out[at] = value.astype(jnp.bfloat16)
            faces.put(write, f32(ref[depth]), f32(ref[last - depth]))
    for i in range(last + 1):
        stiff[i], buoy[i] = coefficients(f32(speed[i]), f32(imped[i]))


def cut_kernel(steps, layers, src, stiff, buoy, loads, fluxes, pressure, velocity):
    y, lanes = stiff.shape[1:]
    write = rows_writer(y)
    run_cut(
        Block((y, lanes), None), steps, layers, lambda k, i: brick_block(src, steps - 1 - k, i),
        lambda i: stiff[i], lambda i: buoy[i], Layers(pressure), Layers(velocity),
        lambda k, a: write(loads, k, a), lambda k, a: write(fluxes, k, a),
    )


def edge_kernel(
    steps, layers, gy_size, own, left, right, loads, fluxes, near, far, strips, whole, series, columns
):
    y, lanes = own.shape[2], loads.shape[1]
    rows = layers * EDGE
    me = lax.axis_index("gy")
    shape = (layers * WIDE, 2 * rows)
    r, c = iota(shape, 0), iota(shape, 1)
    inside = r & (WIDE - 1)
    at = (r >> 5) * EDGE + (r & 3)
    wanted = (inside < EDGE) & (c == at) & (me > 0)
    wanted = wanted | ((inside >= WIDE - EDGE) & (c == rows + at) & (me < gy_size - 1))
    order = jnp.where(wanted, 1.0, 0.0).astype(jnp.bfloat16)

    def narrow(a):
        half = STRIP // 2
        return jnp.concatenate([a[:half], a[WIDE - half :]], 0)

    for f in range(steps + 4):
        parts = jnp.concatenate([a[f * rows : (f + 1) * rows, :] for a in (left, right)], 0)
        whole[f] = own[f] + jnp.dot(order, parts, preferred_element_type=jnp.float32)
        for i in range(layers):
            strips[f, i * STRIP : (i + 1) * STRIP, :] = narrow(whole[f, i * WIDE : (i + 1) * WIDE, :])

    def strip(f, i):
        return whole[f, i * WIDE : (i + 1) * WIDE, :]

    faces = Faces(far, near)
    step, base, _ = strip_layout(steps, y)
    coef = [coefficients(strip(steps, i), strip(steps + 1, i)) for i in range(layers)]
    strip_loads, strip_fluxes = {}, {}
    run_cut(
        Strip((WIDE, y), None), steps, layers, lambda k, i: strip(steps - 1 - k, i),
        lambda i: coef[i][0], lambda i: coef[i][1], {}, {}, strip_loads.__setitem__, strip_fluxes.__setitem__,
    )
    outer = EDGE - 1
    series[...] = jnp.zeros(series.shape, jnp.float32)
    for k in range(steps):
        pair = narrow(strip_loads[k]), narrow(strip_fluxes[k])
        faces.put(lambda ref, value: put_strip(ref, base + k * step, value), *pair)
        if k > 0:
            for side, a in enumerate(pair):
                at = outer_key(k, side)
                series[at : at + outer, :] = a[HIGH - outer : HIGH, :]
                series[at + outer : at + 2 * outer, :] = a[LOW + 1 : LOW + 1 + outer, :]
    columns[...] = series[...].T

    lane = iota((y, lanes), 1)
    read, write = rows_reader(y), rows_writer(y)

    def merged(ref, k, side):
        a = read(k)(ref)
        if k == 0:
            return a
        placed = pltpu.roll(columns[...], (lanes - outer - outer_key(k, side)) % lanes, 1)
        return jnp.where((lane < k) | (lane >= lanes - k), placed, a)

    for k in range(steps):
        faces.put(lambda ref, value: write(ref, k, value), merged(loads, k, 0), merged(fluxes, k, 1))


def outer_key(step, side):
    return ((step - 1) * 2 + side) * 8


def joined_kernel(
    steps, layers, src, stiff, buoy, strips, near, far, coef_near, coef_far, pressure_out, velocity_out,
    pressure, velocity, series, columns, sems,
):
    y, lanes = stiff.shape[1:]

    def strip(f, i):
        return strips[f, i * STRIP : (i + 1) * STRIP, :]

    faces = Faces(far, near)
    step, base, _ = strip_layout(steps, y)
    held = Faces(coef_far, coef_near)
    edge_held = Faces(steps + 3, steps + 2)

    def strip_at(at):
        return lambda ref: strip_rows(ref, at, y)

    def beside(side, at):
        s = [side(at(j)) for j in range(4)]
        (stiff, buoy), (stiff2, buoy2) = coefficients(s[0], s[2]), coefficients(s[1], s[3])
        return stiff, stiff2, buoy, buoy2

    coef = [coefficients(strip(steps, i), strip(steps + 1, i)) for i in range(layers)]
    series[...] = jnp.zeros(series.shape, jnp.float32)
    run_joined(
        Strip((STRIP, y), series), steps, layers, lambda k, i: strip(steps - 1 - k, i),
        lambda i: coef[i][0], lambda i: coef[i][1], {}, {},
        lambda k: faces.above(strip_at(base + k * step)), lambda k: faces.below(strip_at(base + k * step)),
        beside(edge_held.above, lambda j: lambda f: strip(f, j)),
        beside(edge_held.below, lambda j: lambda f: strip(f, j)),
    )
    columns[...] = series[...].T

    def copies(i):
        return (
            pltpu.make_async_copy(velocity.at[:, i], velocity_out.at[:, i], sems.at[0, i]),
            pltpu.make_async_copy(pressure.at[i], pressure_out.at[i], sems.at[1, i]),
        )

    def send(i):
        for copy in copies(i):
            copy.start()

    read = rows_reader(y)
    run_joined(
        Block((y, lanes), columns), steps, layers, lambda k, i: brick_block(src, steps - 1 - k, i),
        lambda i: stiff[i], lambda i: buoy[i], Layers(pressure), Layers(velocity),
        lambda k: faces.above(read(k)), lambda k: faces.below(read(k)),
        beside(held.above, lambda j: lambda ref: f32(ref[j])),
        beside(held.below, lambda j: lambda ref: f32(ref[j])),
        send,
    )
    for i in range(layers):
        for copy in copies(i):
            copy.wait()


def shifted(block, axis, distance):
    devices = range(lax.axis_size(axis))
    return lax.ppermute(block, axis, [(i, i + distance) for i in devices if i + distance in devices])


def swapped(block, axis, first):
    pairs = [(i, i + 1) for i in range(first, lax.axis_size(axis) - 1, 2)]
    return lax.ppermute(block, axis, pairs + [(j, i) for i, j in pairs])


def on_device(source, speed, impedance):
    steps, whole_x, brick_y, lanes = source.shape
    layers, y, _ = speed.shape
    assert layers == steps == EDGE and lanes == 128 and y % 128 == 0
    gy_size = lax.axis_size("gy")
    xs = ("grp", "gx")
    bf16 = jnp.bfloat16
    params = pltpu.CompilerParams(vmem_limit_bytes=32 * 1024 * 1024)
    sds = jax.ShapeDtypeStruct

    assert lax.axis_size("gx") % 2 == 0
    field, coef = sds((layers, y, lanes), jnp.float32), sds((4, y, lanes), bf16)
    stiff, buoy, coef_near, coef_far = pl.pallas_call(
        coefficients_kernel, out_shape=(field, field, coef, coef), compiler_params=params, name="coefficients"
    )(speed, impedance)
    coef_near, coef_far = swapped(coef_near, xs, 0), swapped(coef_far, xs, 1)
    relaid = lax.all_to_all(source.transpose(1, 0, 2, 3), xs, split_axis=0, concat_axis=0, tiled=True)
    relaid = relaid.reshape(whole_x // layers, layers, steps, brick_y, lanes)
    relaid, coef_near, coef_far, stiff, buoy = lax.optimization_barrier((relaid, coef_near, coef_far, stiff, buoy))

    def call(kernel, outs, scratch, *args, name):
        return pl.pallas_call(kernel, out_shape=outs, scratch_shapes=scratch, compiler_params=params, name=name)(*args)

    edge = sds(((steps + 4) * layers * EDGE, y), bf16)
    fields = relaid, speed, impedance, coef_near, coef_far
    low, high = call(functools.partial(pack_kernel, steps, layers), (edge, edge), [], *fields, name="pack")
    if gy_size == 2:
        left = right = lax.ppermute(jnp.where(lax.axis_index("gy") == 0, high, low), "gy", [(0, 1), (1, 0)])
    else:
        left, right = shifted(high, "gy", 1), shifted(low, "gy", -1)

    own = call(
        functools.partial(own_kernel, steps, layers), sds((steps + 4, layers * WIDE, y), jnp.float32), [], *fields, name="own"
    )
    whole = pltpu.VMEM((layers, y, lanes), jnp.float32)
    whole_velocity = pltpu.VMEM((3, layers, y, lanes), jnp.float32)
    series = [pltpu.VMEM((128, y), jnp.float32), pltpu.VMEM((y, 128), jnp.float32)]
    face = sds((steps * y, 128), bf16)
    loads, fluxes = call(
        functools.partial(cut_kernel, steps, layers), (face, face), [whole, whole_velocity], relaid, stiff, buoy, name="cut"
    )
    message = sds((strip_layout(steps, y)[2], 128), bf16)
    near, far, strips = call(
        functools.partial(edge_kernel, steps, layers, gy_size),
        (message, message, sds((steps + 4, layers * STRIP, y), jnp.float32)),
        [pltpu.VMEM((steps + 4, layers * WIDE, y), jnp.float32)] + series,
        own, left, right, loads, fluxes, name="edge",
    )
    near = swapped(near, xs, 0)
    far = swapped(far, xs, 1)

    args = relaid, stiff, buoy, strips, near, far, coef_near, coef_far
    return pl.pallas_call(
        functools.partial(joined_kernel, steps, layers),
        in_specs=[pl.BlockSpec(memory_space=pltpu.VMEM)] * len(args),
        out_specs=(pl.BlockSpec(memory_space=pl.ANY), pl.BlockSpec(memory_space=pl.ANY)),
        out_shape=(field, sds((3, layers, y, lanes), jnp.float32)),
        scratch_shapes=[whole, whole_velocity] + series + [pltpu.SemaphoreType.DMA((2, layers))],
        compiler_params=params,
        name="joined",
    )(*args)


def solution(mesh):
    in_specs = (
        P(None, None, ("grp", "gx"), "gy"),
        P(("grp", "gx"), None, "gy"),
        P(("grp", "gx"), None, "gy"),
    )
    out_specs = (P(("grp", "gx"), None, "gy"), P(None, ("grp", "gx"), None, "gy"))
    return jax.shard_map(
        on_device, mesh=mesh, in_specs=in_specs, out_specs=out_specs, check_vma=False
    )
```
